32 devices in a mesh: dp: 2 (over y), expert: 16 (over z, x, core).
Axes of the slice: x: 2, y: 2, z: 4, core: 2. Of those that a mesh axis runs over, the one named last changes fastest.
Arguments:
- tokens: bfloat16 [1024, 4096], P('expert', 'dp'), may hold values from -6 to 6
- expert_ids: int32 [1024, 8], P('expert'), may hold values from 0 to 15, all different within a row; in each aligned block of 64 rows (0 to 63, 64 to 127, ...) at most 64 rows name the same one
- gate_weights: float32 [1024, 8], P('expert'), may hold values from 0.05 to 1
- gate_proj: bfloat16 [16, 4096, 1536], P('expert', 'dp'), may hold values from -0.09375 to 0.09375
- up_proj: bfloat16 [16, 4096, 1536], P('expert', 'dp'), may hold values from -0.09375 to 0.09375
- down_proj: bfloat16 [16, 1536, 4096], P('expert', None, 'dp'), may hold values from -0.15625 to 0.15625
Outputs:
- combined: bfloat16 [1024, 4096], P('expert', 'dp')
The draws below stay inside these ranges and needn't reach their ends.
Inputs may be any that keep to these rules, and one draw needn't show every extreme that they name: `expert_ids`: each row names 8 different experts. Among the 64 rows of one device (one aligned block), no expert is named by more than 64 rows, and in every draw some expert is named by exactly 64 rows of some block.
All inputs are finite; a program needn't handle non-finite values.
Results may differ from the reference program's by a relative error of at most 0.029.
Values may be sent and summed in bfloat16 or wider, within the bound.
No kernel may reach another device: no remote copies, remote signals or barrier semaphores. Data moves between devices by JAX's collectives and lax.ppermute only.
A program may use at most 64 MiB of HBM per device.

```python
import math
import jax
import jax.numpy as jnp
import numpy as np
from jax import lax

D = 4096
FF = 1536
TOPK = 8
TOK_DEV = 64
EXPERTS = 16
CAP = 64
TOKENS = 1024
N_DP = 2
N_EXPERT = 16


def block_levels(stream_key, shape, shards, low, top_value):
    def one(dim, shards_of):
        heights = jax.random.uniform(jax.random.fold_in(jax.random.fold_in(stream_key, 6), dim), (shards_of,), jnp.float32, low / len(shards), top_value / len(shards))
        return jnp.repeat(jnp.exp(heights), shape[dim] // shards_of).reshape((-1,) + (1,) * (len(shape) - dim - 1))

    level = one(*shards[0])
    for cut in shards[1:]:
        level = level * one(*cut)
    return level


def assign_block(stream_key, own, number, rows, amount, top, reach, skew):
    order = jax.random.permutation(stream_key, amount)
    crowded, ordinary = shares(amount, rows * top, reach, skew, True), shares(amount, rows * top, reach, skew, False)
    places = jnp.arange(amount)

    def named(tallies, offset_by):
        used = int((tallies > 0).sum())
        fixed = max(1, used // 4)
        moved = fixed + (places - fixed + offset_by * (used - fixed)) % max(1, amount - fixed)
        return jnp.zeros((amount,), jnp.int32).at[order[jnp.where(places < fixed, places, moved)]].set(jnp.asarray(tallies, jnp.int32))

    tallies = jnp.where(number % 4 == 0, named(crowded, number // 4), named(ordinary, number - number // 4 - 1))
    mixed = jax.random.permutation(jax.random.fold_in(own, 3), amount)
    source_of, taker = mixed[0:amount // 2 * 2:2], mixed[1:amount // 2 * 2:2]
    room = jnp.minimum(tallies[source_of] - 1, reach - tallies[taker]) // 2
    room = jnp.where((source_of == order[0]) | (taker == order[0]) | (tallies[taker] == 0), 0, jnp.maximum(room, 0))
    moved = jax.random.randint(jax.random.fold_in(own, 4), (amount // 2,), 0, 1 << 20) % (room + 1)
    tallies = tallies.at[source_of].add(-moved).at[taker].add(moved)
    members = jnp.searchsorted(jnp.cumsum(tallies), jnp.arange(rows * top), side="right").astype(jnp.int32)
    table = members.reshape(top, rows).T
    table = table[jax.random.permutation(jax.random.fold_in(own, 1), rows)]
    offset_by = jax.random.randint(jax.random.fold_in(own, 2), (rows, 1), 0, top)
    return jnp.take_along_axis(table, (jnp.arange(top)[None, :] + offset_by) % top, axis=1)


def shares(amount, total, reach, slope, full):
    weights = [(1 << 20) // math.isqrt(standing ** slope) + 1 for standing in range(1, amount + 1)]
    largest = reach if full else min(reach, max(-(-total // amount), total * weights[0] // sum(weights)))
    least = 1 if total - largest >= amount - 1 else 0
    holding, spare = [largest] + [least] * (amount - 1), total - largest - least * (amount - 1)
    while spare > 0:
        candidates = [i for i in range(1, amount) if holding[i] < largest] or [i for i in range(1, amount) if holding[i] < reach]
        pool, left = sum([weights[i] for i in candidates]), spare
        for i in candidates:
            addition = min(reach - holding[i], max(1, left * weights[i] // pool), spare)
            holding[i] = holding[i] + addition
            spare = spare - addition
    return np.array(holding)


def noise(stream_key, extent, scale, reach, split=(), held_as=jnp.bfloat16):
    result = jax.random.normal(stream_key, extent, jnp.float32) * scale
    if len(split) > 0:
        result = block_levels(stream_key, extent, split, -0.22, 0.18) * result
    return jnp.clip(result, min=-reach, max=reach).astype(held_as)


def setup_inputs(seed: int = 0) -> dict:
    keys = jax.random.split(jax.random.key(seed), 7)
    tokens = noise(keys[0], (TOKENS, D), 1.0, 6.0, ((0, 16), (1, 2)))
    expert_ids_keys = jax.random.split(jax.random.fold_in(keys[1], 1), TOKENS // TOK_DEV)
    expert_ids_turns = jax.random.permutation(jax.random.fold_in(keys[1], 3), TOKENS // TOK_DEV)
    expert_ids = jax.vmap(lambda own, number: assign_block(jax.random.fold_in(keys[1], 2), own, number, TOK_DEV, EXPERTS, TOPK, CAP, 2))(expert_ids_keys, expert_ids_turns).reshape((TOKENS, TOPK))
    gate_weights = jnp.clip(jnp.exp(math.log(1.0) - 2.9957323 * jax.random.uniform(keys[2], (TOKENS, TOPK), jnp.float32) ** block_levels(keys[2], (TOKENS, TOPK), ((0, 16),), -0.2, 0.2)), 0.05, 1.0)
    gate_proj = noise(keys[3], (EXPERTS, D, FF), D ** -0.5, 0.09375, ((0, 16), (1, 2)))
    up_proj = noise(keys[4], (EXPERTS, D, FF), D ** -0.5, 0.09375, ((0, 16), (1, 2)))
    down_proj = noise(keys[5], (EXPERTS, FF, D), FF ** -0.5, 0.15625, ((0, 16), (2, 2)))
    return {"tokens": tokens, "expert_ids": expert_ids, "gate_weights": gate_weights, "gate_proj": gate_proj, "up_proj": up_proj, "down_proj": down_proj}


def block_places(block_ids, expert_count, capacity):
    tok_count, top_count = block_ids.shape
    flat_ids = block_ids.reshape(tok_count * top_count)
    matches = (flat_ids[:, None] == jnp.arange(expert_count, dtype=jnp.int32)[None, :]).astype(jnp.int32)
    earlier = jnp.cumsum(matches, axis=0) - matches
    slot_index = jnp.sum(earlier * matches, axis=1)
    return (flat_ids * capacity + slot_index).reshape(tok_count, top_count)


def reference(tokens, expert_ids, gate_weights, gate_proj, up_proj, down_proj):
    shard_width = D // N_DP
    id_blocks = expert_ids.reshape(N_EXPERT, TOK_DEV, TOPK)

    def place_one(block_ids):
        return block_places(block_ids, EXPERTS, CAP)

    places = jax.vmap(place_one)(id_blocks)
    source_tokens = tokens.astype(jnp.float32).reshape(N_EXPERT, TOK_DEV, D)
    route_weights = gate_weights.reshape(N_EXPERT, TOK_DEV, TOPK)
    slot_range = jnp.arange(CAP, dtype=jnp.int32)

    def one_expert(totals, expert_index):
        targets = expert_index * CAP + slot_range
        matches = places[:, :, :, None] == targets[None, None, None, :]
        chosen = jnp.any(matches, axis=2).astype(jnp.float32)
        weighting = jnp.sum(jnp.where(matches, route_weights[:, :, :, None], 0.0), axis=2)
        row_block = jnp.einsum('stc,std->scd', chosen, source_tokens, precision=lax.Precision.HIGHEST)
        pieces = row_block.reshape(N_EXPERT * CAP, N_DP, shard_width)
        gate_w = gate_proj[expert_index].astype(jnp.float32).reshape(N_DP, shard_width, FF)
        up_w = up_proj[expert_index].astype(jnp.float32).reshape(N_DP, shard_width, FF)
        gate_part = jnp.einsum('rjd,jdf->rjf', pieces, gate_w, precision=lax.Precision.HIGHEST)
        up_part = jnp.einsum('rjd,jdf->rjf', pieces, up_w, precision=lax.Precision.HIGHEST)
        gate_part = lax.optimization_barrier(gate_part.astype(jnp.bfloat16))
        up_part = lax.optimization_barrier(up_part.astype(jnp.bfloat16))
        gate_sum = jnp.sum(gate_part.astype(jnp.float32), axis=1)
        up_sum = jnp.sum(up_part.astype(jnp.float32), axis=1)
        hidden = (jax.nn.silu(gate_sum) * up_sum).astype(jnp.bfloat16)
        expert_out = jnp.dot(hidden, down_proj[expert_index], preferred_element_type=jnp.float32).astype(jnp.bfloat16)
        out_block = expert_out.astype(jnp.float32).reshape(N_EXPERT, CAP, D)
        added = jnp.einsum('stc,scd->std', weighting, out_block, precision=lax.Precision.HIGHEST)
        return totals + added, None

    start = jnp.zeros((N_EXPERT, TOK_DEV, D), jnp.float32)
    totals, unused = lax.scan(one_expert, start, jnp.arange(EXPERTS, dtype=jnp.int32))
    return totals.reshape(TOKENS, D).astype(jnp.bfloat16)
```

```python
import jax
import jax.numpy as jnp
from jax import lax
from jax.sharding import PartitionSpec as P


def block_places(block_ids, expert_count, capacity):
    tok_count, top_count = block_ids.shape
    flat_ids = block_ids.reshape(tok_count * top_count)
    matches = (flat_ids[:, None] == jnp.arange(expert_count, dtype=jnp.int32)[None, :]).astype(
        jnp.int32
    )
    earlier = jnp.cumsum(matches, axis=0) - matches
    slot_index = jnp.sum(earlier * matches, axis=1)
    return (flat_ids * capacity + slot_index).reshape(tok_count, top_count)


def dispatch_body(tokens, expert_ids, gate_weights, gate_proj, up_proj, down_proj):
    tok_count, top_count = expert_ids.shape
    row_width = tokens.shape[1]
    sources = lax.axis_size("expert")
    capacity = 2 * tok_count * top_count // sources
    positions = jnp.arange(sources * capacity, dtype=jnp.int32)
    places = block_places(expert_ids, sources, capacity)
    matches = places[:, :, None] == positions[None, None, :]
    weighting = jnp.sum(jnp.where(matches, gate_weights[:, :, None], 0.0), axis=1)
    chosen = jnp.any(matches, axis=1).astype(jnp.bfloat16)
    outgoing = lax.dot_general(
        chosen, tokens, (((0,), (0,)), ((), ())), preferred_element_type=jnp.float32
    ).astype(jnp.bfloat16)
    incoming = lax.all_to_all(
        outgoing.reshape(sources, capacity, row_width),
        "expert",
        split_axis=0,
        concat_axis=0,
        tiled=True,
    )
    expert_rows = incoming.reshape(sources * capacity, row_width)
    gate_part = jnp.dot(expert_rows, gate_proj[0], preferred_element_type=jnp.float32)
    up_part = jnp.dot(expert_rows, up_proj[0], preferred_element_type=jnp.float32)
    gate_sum, up_sum = (
        lax.psum(gate_part.astype(jnp.bfloat16), "dp").astype(jnp.float32),
        lax.psum(up_part.astype(jnp.bfloat16), "dp").astype(jnp.float32),
    )
    hidden = (jax.nn.silu(gate_sum) * up_sum).astype(jnp.bfloat16)
    expert_out = jnp.dot(hidden, down_proj[0], preferred_element_type=jnp.float32).astype(
        jnp.bfloat16
    )
    returned = lax.all_to_all(
        expert_out.reshape(sources, capacity, row_width),
        "expert",
        split_axis=0,
        concat_axis=0,
        tiled=True,
    )
    returned_flat = returned.reshape(sources * capacity, row_width)
    weight_high = weighting.astype(jnp.bfloat16)
    weight_low = (weighting - weight_high.astype(jnp.float32)).astype(jnp.bfloat16)
    combined = jnp.dot(weight_high, returned_flat, preferred_element_type=jnp.float32)
    combined = combined + jnp.dot(weight_low, returned_flat, preferred_element_type=jnp.float32)
    return combined.astype(jnp.bfloat16)


def gather_body(tokens, expert_ids, gate_weights, gate_proj, up_proj, down_proj):
    rows = tokens.shape[0]
    sources = lax.axis_size("expert")
    half = gate_proj.shape[2] // 2
    me = lax.axis_index("expert")
    low = lax.axis_index("dp") == 0
    gate, up, down = gate_proj[0], up_proj[0], down_proj[0]

    def swap(value, r):
        return lax.ppermute(value, "expert", [(i, i ^ r) for i in range(sources)])

    def cross(value):
        return lax.ppermute(value, "dp", [(0, 1), (1, 0)])

    names = jnp.arange(sources, dtype=jnp.int32)
    own_weights = jnp.sum(
        jnp.where(expert_ids[:, :, None] == names, gate_weights[:, :, None], 0.0), axis=1
    )
    all_weights = lax.all_gather(own_weights, "expert", axis=0)
    my_weights = jnp.sum(jnp.where(names == me, all_weights, 0.0), axis=2)

    held = {0: tokens}
    for r in range(4, sources, 4):
        held[r] = swap(tokens, r)
    for r in range(0, sources, 4):
        held[r + 2] = swap(held[r], 2)
    for r in range(0, sources, 4):
        pair = swap(jnp.concatenate([held[r], held[r + 2]]), 1)
        held[r + 1], held[r + 3] = pair[:rows], pair[rows:]

    def partials(blocks):
        chunk = jnp.concatenate([held[r] for r in blocks])
        gate_part = jnp.dot(chunk, gate, preferred_element_type=jnp.float32)
        up_part = jnp.dot(chunk, up, preferred_element_type=jnp.float32)
        kept, sent = [], []
        for part in (gate_part, up_part):
            first, second = part[:, :half], part[:, half:]
            kept.append(jnp.where(low, first, second))
            sent.append(jnp.where(low, second, first).astype(jnp.bfloat16))
        return kept, cross(jnp.concatenate(sent, axis=1))

    def hidden_half(kept, arrived):
        gate_sum = kept[0] + arrived[:, :half].astype(jnp.float32)
        up_sum = kept[1] + arrived[:, half:].astype(jnp.float32)
        return (jax.nn.silu(gate_sum) * up_sum).astype(jnp.bfloat16)

    def outputs(blocks, mine, other):
        hidden = jnp.concatenate(
            [jnp.where(low, mine, other), jnp.where(low, other, mine)], axis=1
        )
        out = jnp.dot(hidden, down, preferred_element_type=jnp.float32)
        return {
            r: out[i * rows : (i + 1) * rows]
            * lax.dynamic_index_in_dim(my_weights, me ^ r, 0, keepdims=False)[:, None]
            for i, r in enumerate(blocks)
        }

    chunks = [[0], [4, 5]]
    chunks += [[r, r + 1, r + 2, r + 3] for r in range(8, sources, 4)]
    chunks += [[6, 7], [2, 3], [1]]

    added = {}
    for blocks in chunks:
        kept, arrived = partials(blocks)
        mine = hidden_half(kept, arrived)
        other = cross(mine)
        added.update(outputs(blocks, mine, other))

    def send(value, r):
        return swap(value.astype(jnp.bfloat16), r).astype(jnp.float32)

    for blocks in chunks:
        odd = [r for r in blocks if r % 2 == 1]
        if not odd:
            continue
        arrived = send(jnp.concatenate([added[r] for r in odd]), 1)
        for i, r in enumerate(odd):
            added[r - 1] = added[r - 1] + arrived[i * rows : (i + 1) * rows]
    total = None
    for r in list(range(8, sources, 4)) + [4, 0]:
        part = added[r] + send(added[r + 2], 2)
        if r > 0:
            part = send(part, r)
        total = part if total is None else total + part
    return total.astype(jnp.bfloat16)


def solution(mesh):
    placed = (
        P("expert", "dp"),
        P("expert", None),
        P("expert", None),
        P("expert", "dp", None),
        P("expert", "dp", None),
        P("expert", None, "dp"),
    )

    def body(tokens, expert_ids, gate_weights, gate_proj, up_proj, down_proj):
        tok_count, top_count = expert_ids.shape
        sources = lax.axis_size("expert")
        whole_blocks = 2 * tok_count * top_count >= sources * tok_count
        paired = lax.axis_size("dp") == 2 and sources >= 8 and sources & (sources - 1) == 0
        plan = gather_body if whole_blocks and paired else dispatch_body
        return plan(tokens, expert_ids, gate_weights, gate_proj, up_proj, down_proj)

    return jax.shard_map(
        body, mesh=mesh, in_specs=placed, out_specs=P("expert", "dp"), check_vma=False
    )
```

```python
import functools

import jax
import jax.numpy as jnp
from jax import lax
from jax.experimental import pallas as pl
from jax.experimental.pallas import tpu as pltpu
from jax.sharding import PartitionSpec as P


def block_places(block_ids, expert_count, capacity):
    tok_count, top_count = block_ids.shape
    flat_ids = block_ids.reshape(tok_count * top_count)
    matches = (flat_ids[:, None] == jnp.arange(expert_count, dtype=jnp.int32)[None, :]).astype(
        jnp.int32
    )
    earlier = jnp.cumsum(matches, axis=0) - matches
    slot_index = jnp.sum(earlier * matches, axis=1)
    return (flat_ids * capacity + slot_index).reshape(tok_count, top_count)


def dispatch_body(tokens, expert_ids, gate_weights, gate_proj, up_proj, down_proj):
    tok_count, top_count = expert_ids.shape
    row_width = tokens.shape[1]
    sources = lax.axis_size("expert")
    capacity = 2 * tok_count * top_count // sources
    positions = jnp.arange(sources * capacity, dtype=jnp.int32)
    places = block_places(expert_ids, sources, capacity)
    matches = places[:, :, None] == positions[None, None, :]
    weighting = jnp.sum(jnp.where(matches, gate_weights[:, :, None], 0.0), axis=1)
    chosen = jnp.any(matches, axis=1).astype(jnp.bfloat16)
    outgoing = lax.dot_general(
        chosen, tokens, (((0,), (0,)), ((), ())), preferred_element_type=jnp.float32
    ).astype(jnp.bfloat16)
    incoming = lax.all_to_all(
        outgoing.reshape(sources, capacity, row_width),
        "expert",
        split_axis=0,
        concat_axis=0,
        tiled=True,
    )
    expert_rows = incoming.reshape(sources * capacity, row_width)
    gate_part = jnp.dot(expert_rows, gate_proj[0], preferred_element_type=jnp.float32)
    up_part = jnp.dot(expert_rows, up_proj[0], preferred_element_type=jnp.float32)
    gate_sum, up_sum = (
        lax.psum(gate_part.astype(jnp.bfloat16), "dp").astype(jnp.float32),
        lax.psum(up_part.astype(jnp.bfloat16), "dp").astype(jnp.float32),
    )
    hidden = (jax.nn.silu(gate_sum) * up_sum).astype(jnp.bfloat16)
    expert_out = jnp.dot(hidden, down_proj[0], preferred_element_type=jnp.float32).astype(
        jnp.bfloat16
    )
    returned = lax.all_to_all(
        expert_out.reshape(sources, capacity, row_width),
        "expert",
        split_axis=0,
        concat_axis=0,
        tiled=True,
    )
    returned_flat = returned.reshape(sources * capacity, row_width)
    weight_high = weighting.astype(jnp.bfloat16)
    weight_low = (weighting - weight_high.astype(jnp.float32)).astype(jnp.bfloat16)
    combined = jnp.dot(weight_high, returned_flat, preferred_element_type=jnp.float32)
    combined = combined + jnp.dot(weight_low, returned_flat, preferred_element_type=jnp.float32)
    return combined.astype(jnp.bfloat16)


LANES = 128
MIB = 1024 * 1024
VMEM_LIMIT = 16 * MIB
TOKEN = jax.ShapeDtypeStruct((8, LANES), jnp.float32)
HERE = pl.BlockSpec(memory_space=pltpu.VMEM)
FAR = pl.BlockSpec(memory_space=pltpu.HBM)


def call(kernel, inputs, outputs, after, scratch=(), relays=(), room=VMEM_LIMIT):
    inputs = [v if isinstance(v, tuple) else (v, HERE) for v in inputs]
    flat = [value for group in relays for value in group]
    joined = [
        jax.ShapeDtypeStruct((sum(v.shape[0] for v in group),) + group[0].shape[1:], group[0].dtype)
        for group in relays
    ]

    def run(*refs):
        refs = list(refs)
        taken = [refs.pop(0) for _ in inputs]
        carried = [refs.pop(0) for _ in flat]
        refs.pop(0)
        made = [refs.pop(0) for _ in outputs]
        joined_refs = [refs.pop(0) for _ in joined]
        token_ref = refs.pop(0)
        token_ref[...] = jnp.zeros(token_ref.shape, token_ref.dtype)
        for group, out_ref in zip(relays, joined_refs, strict=True):
            start = 0
            for _ in group:
                piece = carried.pop(0)
                out_ref[start : start + piece.shape[0], :] = piece[...]
                start += piece.shape[0]
        if kernel is not None:
            kernel(*taken, *made, *refs)

    results = pl.pallas_call(
        run,
        in_specs=[spec for _, spec in inputs] + [HERE] * len(flat) + [pl.BlockSpec(memory_space=pl.ANY)],
        out_specs=[HERE] * (len(outputs) + len(joined) + 1),
        out_shape=list(outputs) + joined + [TOKEN],
        scratch_shapes=list(scratch),
        compiler_params=pltpu.CompilerParams(vmem_limit_bytes=room),
        cost_estimate=pl.CostEstimate(flops=100_000_000_000, bytes_accessed=1, transcendentals=0),
    )(*[value for value, _ in inputs], *flat, after)
    return results[:-1], results[-1]


def label_kernel(sources, tokens_ref, ids_ref, weights_ref, out_ref):
    rows, width = tokens_ref.shape
    out_ref[:, :width] = tokens_ref[...]
    place = lax.broadcasted_iota(jnp.int32, (LANES, rows), 0)
    weight = jnp.zeros((LANES, rows), jnp.float32)
    for k in range(ids_ref.shape[0]):
        weight += jnp.where(ids_ref[k : k + 1, :] == place % sources, weights_ref[k : k + 1, :], 0.0)
    high = weight.astype(jnp.bfloat16).astype(jnp.float32)
    mid = (weight - high).astype(jnp.bfloat16).astype(jnp.float32)
    low = weight - high - mid
    term = place // sources
    picked = jnp.where(term == 0, high, jnp.where(term == 1, mid, jnp.where(term == 2, low, 0.0)))
    out_ref[:, width:] = jnp.transpose(picked).astype(jnp.bfloat16)


def load_kernel(mine, depth, gate_ref, up_ref, *refs):
    *chunk, held_ref, total_ref, sems = refs
    half = held_ref.shape[2]
    owner = lax.axis_index("dp")
    column = pl.multiple_of((owner if mine else 1 - owner) * half, LANES)
    steps = held_ref.shape[1] // depth
    copies = []
    for n in range(steps):
        for i, ref in enumerate((gate_ref, up_ref)):
            copies.append(
                pltpu.make_async_copy(
                    ref.at[0, pl.ds(n * depth, depth), pl.ds(column, half)],
                    held_ref.at[i, pl.ds(n * depth, depth), :],
                    sems.at[n, i],
                )
            )
            copies[-1].start()
    for n in range(steps):
        for i in range(2):
            copies[2 * n + i].wait()
            if not chunk:
                continue
            tokens_ref, out_ref = chunk
            rows = tokens_ref.shape[0]
            part = jnp.dot(
                tokens_ref[:, n * depth : (n + 1) * depth],
                held_ref[i, n * depth : (n + 1) * depth, :],
                preferred_element_type=jnp.float32,
            )
            if n > 0:
                part += total_ref[i]
            if n < steps - 1:
                total_ref[i] = part
            else:
                out_ref[i * rows : (i + 1) * rows, :] = part.astype(jnp.bfloat16)


def collect(piece_refs, width, chunk_ref):
    start = 0
    for piece in piece_refs:
        chunk_ref[start : start + piece.shape[0], :] = piece[:, :width]
        start += piece.shape[0]


def partial_kernel(pieces, riders, tile, *refs):
    held_ref, *rider_refs, out_ref, chunk_ref = refs[pieces:]
    rows, width = chunk_ref.shape
    collect(refs[:pieces], width, chunk_ref)
    start = 2 * rows
    for ref in rider_refs:
        out_ref[start : start + ref.shape[0], :] = ref[...]
        start += ref.shape[0]

    @pl.loop(0, held_ref.shape[2] // tile)
    def _(n):
        here = pl.ds(pl.multiple_of(n * tile, LANES), tile)
        for i in range(2):
            part = jnp.dot(chunk_ref[...], held_ref[i, :, here], preferred_element_type=jnp.float32)
            out_ref[i * rows : (i + 1) * rows, here] = part.astype(jnp.bfloat16)


def hidden_kernel(pieces, tile, *refs):
    held_ref, arrived_ref, out_ref, chunk_ref = refs[pieces:]
    rows, width = chunk_ref.shape
    collect(refs[:pieces], width, chunk_ref)

    @pl.loop(0, held_ref.shape[2] // tile)
    def _(n):
        here = pl.ds(pl.multiple_of(n * tile, LANES), tile)
        gate_sum, up_sum = (
            jnp.dot(chunk_ref[...], held_ref[i, :, here], preferred_element_type=jnp.float32)
            + arrived_ref[i * rows : (i + 1) * rows, here].astype(jnp.float32)
            for i in range(2)
        )
        out_ref[:, here] = (gate_sum / (1.0 + jnp.exp(-gate_sum)) * up_sum).astype(jnp.bfloat16)


def output_kernel(pieces, sources, tile, behind, *refs):
    mine_ref, other_ref, down_ref = refs[pieces : pieces + 3]
    *out_refs, weight_ref = refs[pieces + 3 :]
    start = 0
    for piece in refs[:pieces]:
        rows = piece.shape[0]
        lane = lax.broadcasted_iota(jnp.int32, (rows, LANES), 1)
        label = piece[:, piece.shape[1] - LANES :].astype(jnp.float32)
        terms = jnp.where(lane % sources == lax.axis_index("expert"), label, 0.0)
        weight_ref[start : start + rows, :] = jnp.sum(terms, axis=1, keepdims=True)
        start += rows
    count, half = mine_ref.shape
    other = other_ref[behind : behind + count, :]
    first = lax.axis_index("dp") * half
    mine_rows = pl.ds(pl.multiple_of(first, LANES), half)
    other_rows = pl.ds(pl.multiple_of(half - first, LANES), half)

    @pl.loop(0, down_ref.shape[2] // tile)
    def _(n):
        here = pl.ds(pl.multiple_of(n * tile, LANES), tile)
        out = jnp.dot(mine_ref[...], down_ref[0, mine_rows, here], preferred_element_type=jnp.float32)
        out += jnp.dot(other, down_ref[0, other_rows, here], preferred_element_type=jnp.float32)
        out *= weight_ref[...]
        start = 0
        for ref in out_refs:
            ref[:, here] = out[start : start + ref.shape[0]].astype(ref.dtype)
            start += ref.shape[0]


def add_kernel(sums, *refs):
    inputs = 1 + max(i for terms in sums for i, _ in terms)
    for terms, out_ref in zip(sums, refs[inputs:], strict=True):
        rows = out_ref.shape[0]
        total = None
        for i, start in terms:
            value = refs[i][start : start + rows, :].astype(jnp.float32)
            total = value if total is None else total + value
        out_ref[...] = total.astype(out_ref.dtype)


def gather_body(tokens, expert_ids, gate_weights, gate_proj, up_proj, down_proj):
    rows, width = tokens.shape
    sources = lax.axis_size("expert")
    half = gate_proj.shape[2] // 2
    tile = 256 if half % 256 == 0 else half
    out_tile = 512 if width % 512 == 0 else width
    depth = 512 if width % 512 == 0 else width

    def swap(value, r):
        return lax.ppermute(value, "expert", [(i, i ^ r) for i in range(sources)])

    def cross(value):
        return lax.ppermute(value, "dp", [(0, 1), (1, 0)])

    def array(shape, dtype=jnp.bfloat16):
        return jax.ShapeDtypeStruct(shape, dtype)

    tail = [jnp.zeros(TOKEN.shape, TOKEN.dtype)]

    def step(kernel, inputs, outputs, scratch=(), relays=(), room=VMEM_LIMIT):
        results, tail[0] = call(kernel, inputs, outputs, tail[0], scratch, relays, room)
        return results

    def count(pieces):
        return sum(p.shape[0] for p in pieces)

    def load(mine, chunk, room):
        made = [array((2 * rows, half))] if chunk else []
        *sent, held = step(
            functools.partial(load_kernel, mine, depth),
            [(gate_proj, FAR), (up_proj, FAR), *chunk],
            made + [array((2, width, half))],
            [pltpu.VMEM((2, rows, half), jnp.float32), pltpu.SemaphoreType.DMA((width // depth, 2))],
            room=room,
        )
        return held, *sent

    def partials(pieces, riders=(), relays=()):
        total = count(pieces)
        sent, *relayed = step(
            functools.partial(partial_kernel, len(pieces), len(riders), tile),
            [*pieces, held_other, *riders],
            [array((2 * total + count(riders), half))],
            [pltpu.VMEM((total, width), jnp.bfloat16)],
            relays,
        )
        return cross(sent), *relayed

    def hidden(pieces, arrived, relays=()):
        total = count(pieces)
        mine, *relayed = step(
            functools.partial(hidden_kernel, len(pieces), tile),
            [*pieces, held_mine, arrived],
            [array((total, half))],
            [pltpu.VMEM((total, width), jnp.bfloat16)],
            relays,
        )
        return mine, *relayed

    def outputs(pieces, mine, arrived, behind, even, relays=()):
        total = count(pieces)
        made = [array((even, width), jnp.float32)] if even else []
        made += [array((total - even, width))] if total > even else []
        results = step(
            functools.partial(output_kernel, len(pieces), sources, out_tile, behind),
            [*pieces, mine, arrived, down_proj],
            made,
            [pltpu.VMEM((total, 1), jnp.float32)],
            relays,
        )
        kept = results[0] if even else None
        back = swap(results[len(made) - 1], 1) if total > even else None
        return kept, back, *results[len(made) :]

    def add(values, *sums, relays=()):
        return step(
            functools.partial(add_kernel, [terms for terms, _ in sums]),
            values,
            [shape for _, shape in sums],
            relays=relays,
        )

    def relay(*groups):
        return step(None, [], [], relays=[list(g) for g in groups])

    one, two, wide = array((rows, width)), array((2 * rows, width)), array((rows, width), jnp.float32)
    whole = [(0, 0), (1, 0)]

    held_other, sent = load(False, [tokens], 52 * MIB)
    y0 = cross(sent)
    (labelled,) = step(
        functools.partial(label_kernel, sources),
        [tokens, expert_ids.T, gate_weights.T],
        [array((rows, width + LANES))],
    )
    b1 = swap(labelled, 1)
    z4, z8 = swap(labelled, 4), swap(labelled, 8)
    (held_mine,) = load(True, [], 46 * MIB)
    (y1,) = partials([b1])
    (b4,) = relay([z4])
    b5, x6 = swap(b4, 1), swap(b4, 2)
    (h0,) = hidden([tokens], y0)
    p2 = [b4, b5]
    y2, again = partials(p2, [h0], relays=[[labelled]])
    z12 = swap(again, 12)
    (b8,) = relay([z8])
    x10 = swap(b8, 2)
    (h1,) = hidden([b1], y1)
    (b8,) = relay([b8, x10])
    b9 = swap(b8, 1)
    b6, again = relay([x6], [labelled])
    b7 = swap(b6, 1)
    p3 = [b8, b9]
    (y3,) = partials(p3, [h1])
    (b12,) = relay([z12])
    x14 = swap(b12, 2)
    h2, again = hidden(p2, y2, relays=[[again]])
    (b12,) = relay([b12, x14])
    b13 = swap(b12, 1)
    c0, _ = outputs([labelled], h0, y2, 4 * rows, rows)
    p4 = [b12, b13]
    y4, again = partials(p4, [h2], relays=[[again]])
    x2 = swap(again, 2)
    (h3,) = hidden(p3, y3)
    p5 = [b6, b7]
    (y5,) = partials(p5, [h3])
    _, c1 = outputs([b1], h1, y3, 8 * rows, 0)
    (b2,) = relay([x2])
    b3 = swap(b2, 1)
    (total,) = add([c0, c1], (whole, wide))
    (h4,) = hidden(p4, y4)
    t4 = cross(h4)
    c4, c5 = outputs(p2, h2, y4, 8 * rows, rows)
    p6 = [b2, b3]
    (y6,) = partials(p6)
    (sent,) = add([c4, c5], (whole, one))
    s4 = swap(sent, 4)
    (h5,) = hidden(p5, y5)
    t5 = cross(h5)
    c8, c9 = outputs(p3, h3, y5, 4 * rows, 2 * rows)
    (total,) = add([total, s4], (whole, wide))
    kept, sent = add([c8, c9], (whole, wide), ([(0, rows), (1, rows)], one))
    x10 = swap(sent, 2)
    c12, c13 = outputs(p4, h4, t4, 0, 2 * rows)
    (sent,) = add([kept, x10], (whole, one))
    s8 = swap(sent, 8)
    kept, sent = add([c12, c13], (whole, wide), ([(0, rows), (1, rows)], one))
    x14 = swap(sent, 2)
    (h6,) = hidden(p6, y6)
    t6 = cross(h6)
    c6, c7 = outputs(p5, h5, t5, 0, rows)
    (sent,) = add([kept, x14], (whole, one))
    s12 = swap(sent, 12)
    (sent,) = add([c6, c7], (whole, one))
    s6 = swap(sent, 6)
    c2, c3 = outputs(p6, h6, t6, 0, rows)
    (total,) = add([total, s8], (whole, wide))
    (sent,) = add([c2, c3], (whole, one))
    s2 = swap(sent, 2)
    (total,) = add([total, s12, s6], (whole + [(2, 0)], wide))
    (total,) = add([total, s2], (whole, one))
    return total


def solution(mesh):
    placed = (
        P("expert", "dp"),
        P("expert", None),
        P("expert", None),
        P("expert", "dp", None),
        P("expert", "dp", None),
        P("expert", None, "dp"),
    )

    def body(tokens, expert_ids, gate_weights, gate_proj, up_proj, down_proj):
        tok_count, top_count = expert_ids.shape
        sources = lax.axis_size("expert")
        whole_blocks = 2 * tok_count * top_count >= sources * tok_count
        paired = lax.axis_size("dp") == 2 and sources == 16
        plan = gather_body if whole_blocks and paired else dispatch_body
        return plan(tokens, expert_ids, gate_weights, gate_proj, up_proj, down_proj)

    return jax.shard_map(
        body, mesh=mesh, in_specs=placed, out_specs=P("expert", "dp"), check_vma=False
    )
```

```python
import functools

import jax
import jax.numpy as jnp
from jax import lax
from jax.experimental import pallas as pl
from jax.experimental.pallas import tpu as pltpu
from jax.sharding import PartitionSpec as P


def block_places(block_ids, expert_count, capacity):
    tok_count, top_count = block_ids.shape
    flat_ids = block_ids.reshape(tok_count * top_count)
    matches = (flat_ids[:, None] == jnp.arange(expert_count, dtype=jnp.int32)[None, :]).astype(
        jnp.int32
    )
    earlier = jnp.cumsum(matches, axis=0) - matches
    slot_index = jnp.sum(earlier * matches, axis=1)
    return (flat_ids * capacity + slot_index).reshape(tok_count, top_count)


def dispatch_body(tokens, expert_ids, gate_weights, gate_proj, up_proj, down_proj):
    tok_count, top_count = expert_ids.shape
    row_width = tokens.shape[1]
    sources = lax.axis_size("expert")
    capacity = 2 * tok_count * top_count // sources
    positions = jnp.arange(sources * capacity, dtype=jnp.int32)
    places = block_places(expert_ids, sources, capacity)
    matches = places[:, :, None] == positions[None, None, :]
    weighting = jnp.sum(jnp.where(matches, gate_weights[:, :, None], 0.0), axis=1)
    chosen = jnp.any(matches, axis=1).astype(jnp.bfloat16)
    outgoing = lax.dot_general(
        chosen, tokens, (((0,), (0,)), ((), ())), preferred_element_type=jnp.float32
    ).astype(jnp.bfloat16)
    incoming = lax.all_to_all(
        outgoing.reshape(sources, capacity, row_width),
        "expert",
        split_axis=0,
        concat_axis=0,
        tiled=True,
    )
    expert_rows = incoming.reshape(sources * capacity, row_width)
    gate_part = jnp.dot(expert_rows, gate_proj[0], preferred_element_type=jnp.float32)
    up_part = jnp.dot(expert_rows, up_proj[0], preferred_element_type=jnp.float32)
    gate_sum, up_sum = (
        lax.psum(gate_part.astype(jnp.bfloat16), "dp").astype(jnp.float32),
        lax.psum(up_part.astype(jnp.bfloat16), "dp").astype(jnp.float32),
    )
    hidden = (jax.nn.silu(gate_sum) * up_sum).astype(jnp.bfloat16)
    expert_out = jnp.dot(hidden, down_proj[0], preferred_element_type=jnp.float32).astype(
        jnp.bfloat16
    )
    returned = lax.all_to_all(
        expert_out.reshape(sources, capacity, row_width),
        "expert",
        split_axis=0,
        concat_axis=0,
        tiled=True,
    )
    returned_flat = returned.reshape(sources * capacity, row_width)
    weight_high = weighting.astype(jnp.bfloat16)
    weight_low = (weighting - weight_high.astype(jnp.float32)).astype(jnp.bfloat16)
    combined = jnp.dot(weight_high, returned_flat, preferred_element_type=jnp.float32)
    combined = combined + jnp.dot(weight_low, returned_flat, preferred_element_type=jnp.float32)
    return combined.astype(jnp.bfloat16)


LANES = 128
VMEM_LIMIT = 10 * 1024 * 1024
COST = 8_000_000_000
COSTS = {}
TOKEN = jax.ShapeDtypeStruct((8, LANES), jnp.float32)
HERE = pl.BlockSpec(memory_space=pltpu.VMEM)


def call(kernel, inputs, outputs, after, scratch=(), relays=(), cost=0):
    inputs = [v if isinstance(v, tuple) else (v, HERE) for v in inputs]
    flat = [value for group in relays for value in group]
    joined = [
        jax.ShapeDtypeStruct((sum(v.shape[0] for v in group),) + group[0].shape[1:], group[0].dtype)
        for group in relays
    ]

    def run(*refs):
        refs = list(refs)
        taken = [refs.pop(0) for _ in inputs]
        carried = [refs.pop(0) for _ in flat]
        refs.pop(0)
        made = [refs.pop(0) for _ in outputs]
        joined_refs = [refs.pop(0) for _ in joined]
        token_ref = refs.pop(0)
        token_ref[...] = jnp.zeros(token_ref.shape, token_ref.dtype)
        for group, out_ref in zip(relays, joined_refs, strict=True):
            start = 0
            for _ in group:
                piece = carried.pop(0)
                out_ref[start : start + piece.shape[0], :] = piece[...]
                start += piece.shape[0]
        if kernel is not None:
            kernel(*taken, *made, *refs)

    results = pl.pallas_call(
        run,
        in_specs=[spec for _, spec in inputs] + [HERE] * len(flat) + [pl.BlockSpec(memory_space=pl.ANY)],
        out_specs=[HERE] * (len(outputs) + len(joined) + 1),
        out_shape=list(outputs) + joined + [TOKEN],
        scratch_shapes=list(scratch),
        compiler_params=pltpu.CompilerParams(vmem_limit_bytes=VMEM_LIMIT),
        cost_estimate=pl.CostEstimate(flops=cost, bytes_accessed=1, transcendentals=0),
    )(*[value for value, _ in inputs], *flat, after)
    return results[:-1], results[-1]


def label_kernel(sources, tokens_ref, ids_ref, weights_ref, out_ref):
    rows, width = tokens_ref.shape
    out_ref[:, :width] = tokens_ref[...]
    place = lax.broadcasted_iota(jnp.int32, (LANES, rows), 0)
    weight = jnp.zeros((LANES, rows), jnp.float32)
    for k in range(ids_ref.shape[0]):
        weight += jnp.where(ids_ref[k : k + 1, :] == place % sources, weights_ref[k : k + 1, :], 0.0)
    high = weight.astype(jnp.bfloat16).astype(jnp.float32)
    mid = (weight - high).astype(jnp.bfloat16).astype(jnp.float32)
    low = weight - high - mid
    term = place // sources
    picked = jnp.where(term == 0, high, jnp.where(term == 1, mid, jnp.where(term == 2, low, 0.0)))
    out_ref[:, width:] = jnp.transpose(picked).astype(jnp.bfloat16)


def collect(piece_refs, width, chunk_ref):
    start = 0
    for piece in piece_refs:
        chunk_ref[start : start + piece.shape[0], :] = piece[:, :width]
        start += piece.shape[0]


def partial_kernel(pieces, riders, tile, *refs):
    gate_ref, up_ref, *rider_refs, out_ref, chunk_ref = refs[pieces:]
    rows, width = chunk_ref.shape
    half = out_ref.shape[1]
    column = (1 - lax.axis_index("dp")) * half
    collect(refs[:pieces], width, chunk_ref)
    start = 2 * rows
    for ref in rider_refs:
        out_ref[start : start + ref.shape[0], :] = ref[...]
        start += ref.shape[0]

    @pl.loop(0, half // tile)
    def _(n):
        here = pl.ds(pl.multiple_of(column + n * tile, LANES), tile)
        there = pl.ds(pl.multiple_of(n * tile, LANES), tile)
        for i, ref in enumerate((gate_ref, up_ref)):
            part = jnp.dot(chunk_ref[...], ref[0, :, here], preferred_element_type=jnp.float32)
            out_ref[i * rows : (i + 1) * rows, there] = part.astype(jnp.bfloat16)


def hidden_kernel(pieces, tile, *refs):
    gate_ref, up_ref, arrived_ref, out_ref, chunk_ref = refs[pieces:]
    rows, width = chunk_ref.shape
    half = out_ref.shape[1]
    column = lax.axis_index("dp") * half
    collect(refs[:pieces], width, chunk_ref)

    @pl.loop(0, half // tile)
    def _(n):
        here = pl.ds(pl.multiple_of(column + n * tile, LANES), tile)
        there = pl.ds(pl.multiple_of(n * tile, LANES), tile)
        gate_sum, up_sum = (
            jnp.dot(chunk_ref[...], ref[0, :, here], preferred_element_type=jnp.float32)
            + arrived_ref[i * rows : (i + 1) * rows, there].astype(jnp.float32)
            for i, ref in enumerate((gate_ref, up_ref))
        )
        out_ref[:, there] = (gate_sum / (1.0 + jnp.exp(-gate_sum)) * up_sum).astype(jnp.bfloat16)


def output_kernel(pieces, sources, tile, behind, *refs):
    mine_ref, other_ref, down_ref = refs[pieces : pieces + 3]
    *out_refs, weight_ref = refs[pieces + 3 :]
    start = 0
    for piece in refs[:pieces]:
        rows = piece.shape[0]
        lane = lax.broadcasted_iota(jnp.int32, (rows, LANES), 1)
        label = piece[:, piece.shape[1] - LANES :].astype(jnp.float32)
        terms = jnp.where(lane % sources == lax.axis_index("expert"), label, 0.0)
        weight_ref[start : start + rows, :] = jnp.sum(terms, axis=1, keepdims=True)
        start += rows
    count, half = mine_ref.shape
    other = other_ref[behind : behind + count, :]
    first = lax.axis_index("dp") * half
    mine_rows = pl.ds(pl.multiple_of(first, LANES), half)
    other_rows = pl.ds(pl.multiple_of(half - first, LANES), half)

    @pl.loop(0, down_ref.shape[2] // tile)
    def _(n):
        here = pl.ds(pl.multiple_of(n * tile, LANES), tile)
        out = jnp.dot(mine_ref[...], down_ref[0, mine_rows, here], preferred_element_type=jnp.float32)
        out += jnp.dot(other, down_ref[0, other_rows, here], preferred_element_type=jnp.float32)
        out *= weight_ref[...]
        start = 0
        for ref in out_refs:
            ref[:, here] = out[start : start + ref.shape[0]].astype(ref.dtype)
            start += ref.shape[0]


def add_kernel(sums, *refs):
    inputs = 1 + max(i for terms in sums for i, _ in terms)
    for terms, out_ref in zip(sums, refs[inputs:], strict=True):
        rows = out_ref.shape[0]
        total = None
        for i, start in terms:
            value = refs[i][start : start + rows, :].astype(jnp.float32)
            total = value if total is None else total + value
        out_ref[...] = total.astype(out_ref.dtype)


def gather_body(tokens, expert_ids, gate_weights, gate_proj, up_proj, down_proj):
    rows, width = tokens.shape
    sources = lax.axis_size("expert")
    half = gate_proj.shape[2] // 2
    tile = 256 if half % 256 == 0 else half
    out_tile = 512 if width % 512 == 0 else width

    def swap(value, r):
        return lax.ppermute(value, "expert", [(i, i ^ r) for i in range(sources)])

    def cross(value):
        return lax.ppermute(value, "dp", [(0, 1), (1, 0)])

    def array(shape, dtype=jnp.bfloat16):
        return jax.ShapeDtypeStruct(shape, dtype)

    tail, number = [jnp.zeros(TOKEN.shape, TOKEN.dtype)], [0]

    def step(kernel, inputs, outputs, scratch=(), relays=()):
        results, tail[0] = call(
            kernel, inputs, outputs, tail[0], scratch, relays, COSTS.get(number[0], COST)
        )
        number[0] += 1
        return results

    def count(pieces):
        return sum(p.shape[0] for p in pieces)

    def partials(pieces, riders=(), relays=()):
        total = count(pieces)
        sent, *relayed = step(
            functools.partial(partial_kernel, len(pieces), len(riders), tile),
            [*pieces, gate_proj, up_proj, *riders],
            [array((2 * total + count(riders), half))],
            [pltpu.VMEM((total, width), jnp.bfloat16)],
            relays,
        )
        return sent, *relayed

    def hidden(pieces, arrived, relays=()):
        total = count(pieces)
        mine, *relayed = step(
            functools.partial(hidden_kernel, len(pieces), tile),
            [*pieces, gate_proj, up_proj, arrived],
            [array((total, half))],
            [pltpu.VMEM((total, width), jnp.bfloat16)],
            relays,
        )
        return mine, *relayed

    def outputs(pieces, mine, arrived, behind, even, relays=()):
        total = count(pieces)
        made = [array((even, width), jnp.float32)] if even else []
        made += [array((total - even, width))] if total > even else []
        results = step(
            functools.partial(output_kernel, len(pieces), sources, out_tile, behind),
            [*pieces, mine, arrived, down_proj],
            made,
            [pltpu.VMEM((total, 1), jnp.float32)],
            relays,
        )
        kept = results[0] if even else None
        back = swap(results[len(made) - 1], 1) if total > even else None
        return kept, back, *results[len(made) :]

    def add(values, *sums, relays=()):
        return step(
            functools.partial(add_kernel, [terms for terms, _ in sums]),
            values,
            [shape for _, shape in sums],
            relays=relays,
        )

    def relay(*groups):
        return step(None, [], [], relays=[list(g) for g in groups])

    one, two, wide = array((rows, width)), array((2 * rows, width)), array((rows, width), jnp.float32)
    whole = [(0, 0), (1, 0)]

    def gap():
        step(None, [], [])

    (labelled,) = step(
        functools.partial(label_kernel, sources),
        [tokens, expert_ids.T, gate_weights.T],
        [array((rows, width + LANES))],
    )
    b1, z4 = swap(labelled, 1), swap(labelled, 4)
    p0 = [labelled, b1]
    (sent,) = partials(p0)
    y0 = cross(sent)
    (again,) = relay([labelled])
    z8 = swap(again, 8)
    (b4,) = relay([z4])
    b5, x6 = swap(b4, 1), swap(b4, 2)
    gap()
    p1 = [b4, b5]
    (sent,) = partials(p1)
    y1 = cross(sent)
    (b6,) = relay([x6])
    b7 = swap(b6, 1)
    (h0,) = hidden(p0, y0)
    p2 = [b6, b7]
    (sent,) = partials(p2, [h0])
    y2 = cross(sent)
    b8, again = relay([z8], [again])
    x10, z12 = swap(b8, 2), swap(again, 12)
    (h1,) = hidden(p1, y1)
    (b8,) = relay([b8, x10])
    b9 = swap(b8, 1)
    gap()
    p3 = [b8, b9]
    (sent,) = partials(p3, [h1])
    y3 = cross(sent)
    (again,) = relay([again])
    x2 = swap(again, 2)
    (h2,) = hidden(p2, y2)
    c0, c1 = outputs(p0, h0, y2, 4 * rows, rows)
    (b12,) = relay([z12])
    x14 = swap(b12, 2)
    (total,) = add([c0, c1], (whole, wide))
    (b12,) = relay([b12, x14])
    b13 = swap(b12, 1)
    gap()
    p4 = [b12, b13]
    (sent,) = partials(p4, [h2])
    y4 = cross(sent)
    (b2,) = relay([x2])
    b3 = swap(b2, 1)
    (h3,) = hidden(p3, y3)
    t3 = cross(h3)
    c4, c5 = outputs(p1, h1, y3, 8 * rows, rows)
    gap()
    (sent,) = add([c4, c5], (whole, one))
    s4 = swap(sent, 4)
    p5 = [b2, b3]
    (later,) = partials(p5)
    (h4,) = hidden(p4, y4)
    t4 = cross(h4)
    total, sent = add([total, s4], (whole, wide), relays=[[later]])
    y5 = cross(sent)
    c6, c7 = outputs(p2, h2, y4, 8 * rows, rows)
    gap()
    (sent,) = add([c6, c7], (whole, one))
    s6 = swap(sent, 6)
    c8, c9 = outputs(p3, h3, t3, 0, 2 * rows)
    gap()
    kept8, sent = add([c8, c9], (whole, wide), ([(0, rows), (1, rows)], one))
    x10 = swap(sent, 2)
    c12, c13 = outputs(p4, h4, t4, 0, 2 * rows)
    (total,) = add([total, s6], (whole, wide))
    kept12, sent = add([c12, c13], (whole, wide), ([(0, rows), (1, rows)], one))
    x14 = swap(sent, 2)
    (sent,) = add([kept8, x10], (whole, one))
    s8 = swap(sent, 8)
    (h5,) = hidden(p5, y5)
    t5 = cross(h5)
    (sent,) = add([kept12, x14], (whole, one))
    s12 = swap(sent, 12)
    c2, c3 = outputs(p5, h5, t5, 0, rows)
    gap()
    (sent,) = add([c2, c3], (whole, one))
    s2 = swap(sent, 2)
    (total,) = add([total, s8], (whole, wide))
    (total,) = add([total, s12, s2], (whole + [(2, 0)], one))
    return total


def solution(mesh):
    placed = (
        P("expert", "dp"),
        P("expert", None),
        P("expert", None),
        P("expert", "dp", None),
        P("expert", "dp", None),
        P("expert", None, "dp"),
    )

    def body(tokens, expert_ids, gate_weights, gate_proj, up_proj, down_proj):
        tok_count, top_count = expert_ids.shape
        sources = lax.axis_size("expert")
        whole_blocks = 2 * tok_count * top_count >= sources * tok_count
        paired = lax.axis_size("dp") == 2 and sources == 16
        plan = gather_body if whole_blocks and paired else dispatch_body
        return plan(tokens, expert_ids, gate_weights, gate_proj, up_proj, down_proj)

    return jax.shard_map(
        body, mesh=mesh, in_specs=placed, out_specs=P("expert", "dp"), check_vma=False
    )
```

```python
import functools

import jax
import jax.numpy as jnp
from jax import lax
from jax.experimental import pallas as pl
from jax.experimental.pallas import tpu as pltpu
from jax.sharding import PartitionSpec as P


def block_places(block_ids, expert_count, capacity):
    tok_count, top_count = block_ids.shape
    flat_ids = block_ids.reshape(tok_count * top_count)
    matches = (flat_ids[:, None] == jnp.arange(expert_count, dtype=jnp.int32)[None, :]).astype(
        jnp.int32
    )
    earlier = jnp.cumsum(matches, axis=0) - matches
    slot_index = jnp.sum(earlier * matches, axis=1)
    return (flat_ids * capacity + slot_index).reshape(tok_count, top_count)


def dispatch_body(tokens, expert_ids, gate_weights, gate_proj, up_proj, down_proj):
    tok_count, top_count = expert_ids.shape
    row_width = tokens.shape[1]
    sources = lax.axis_size("expert")
    capacity = 2 * tok_count * top_count // sources
    positions = jnp.arange(sources * capacity, dtype=jnp.int32)
    places = block_places(expert_ids, sources, capacity)
    matches = places[:, :, None] == positions[None, None, :]
    weighting = jnp.sum(jnp.where(matches, gate_weights[:, :, None], 0.0), axis=1)
    chosen = jnp.any(matches, axis=1).astype(jnp.bfloat16)
    outgoing = lax.dot_general(
        chosen, tokens, (((0,), (0,)), ((), ())), preferred_element_type=jnp.float32
    ).astype(jnp.bfloat16)
    incoming = lax.all_to_all(
        outgoing.reshape(sources, capacity, row_width),
        "expert",
        split_axis=0,
        concat_axis=0,
        tiled=True,
    )
    expert_rows = incoming.reshape(sources * capacity, row_width)
    gate_part = jnp.dot(expert_rows, gate_proj[0], preferred_element_type=jnp.float32)
    up_part = jnp.dot(expert_rows, up_proj[0], preferred_element_type=jnp.float32)
    gate_sum, up_sum = (
        lax.psum(gate_part.astype(jnp.bfloat16), "dp").astype(jnp.float32),
        lax.psum(up_part.astype(jnp.bfloat16), "dp").astype(jnp.float32),
    )
    hidden = (jax.nn.silu(gate_sum) * up_sum).astype(jnp.bfloat16)
    expert_out = jnp.dot(hidden, down_proj[0], preferred_element_type=jnp.float32).astype(
        jnp.bfloat16
    )
    returned = lax.all_to_all(
        expert_out.reshape(sources, capacity, row_width),
        "expert",
        split_axis=0,
        concat_axis=0,
        tiled=True,
    )
    returned_flat = returned.reshape(sources * capacity, row_width)
    weight_high = weighting.astype(jnp.bfloat16)
    weight_low = (weighting - weight_high.astype(jnp.float32)).astype(jnp.bfloat16)
    combined = jnp.dot(weight_high, returned_flat, preferred_element_type=jnp.float32)
    combined = combined + jnp.dot(weight_low, returned_flat, preferred_element_type=jnp.float32)
    return combined.astype(jnp.bfloat16)


LANES = 128
VMEM_LIMIT = 10 * 1024 * 1024
COST = 8_000_000_000
COSTS = {}
TOKEN = jax.ShapeDtypeStruct((8, LANES), jnp.float32)
HERE = pl.BlockSpec(memory_space=pltpu.VMEM)


def call(kernel, inputs, outputs, after, scratch=(), relays=(), cost=0):
    inputs = [v if isinstance(v, tuple) else (v, HERE) for v in inputs]
    flat = [value for group in relays for value in group]
    joined = [
        jax.ShapeDtypeStruct((sum(v.shape[0] for v in group),) + group[0].shape[1:], group[0].dtype)
        for group in relays
    ]

    def run(*refs):
        refs = list(refs)
        taken = [refs.pop(0) for _ in inputs]
        carried = [refs.pop(0) for _ in flat]
        del refs[: len(after)]
        made = [refs.pop(0) for _ in outputs]
        joined_refs = [refs.pop(0) for _ in joined]
        token_ref = refs.pop(0)
        token_ref[...] = jnp.zeros(token_ref.shape, token_ref.dtype)
        for group, out_ref in zip(relays, joined_refs, strict=True):
            start = 0
            for _ in group:
                piece = carried.pop(0)
                out_ref[start : start + piece.shape[0], :] = piece[...]
                start += piece.shape[0]
        if kernel is not None:
            kernel(*taken, *made, *refs)

    results = pl.pallas_call(
        run,
        in_specs=[spec for _, spec in inputs] + [HERE] * len(flat) + [pl.BlockSpec(memory_space=pl.ANY)] * len(after),
        out_specs=[HERE] * (len(outputs) + len(joined) + 1),
        out_shape=list(outputs) + joined + [TOKEN],
        scratch_shapes=list(scratch),
        compiler_params=pltpu.CompilerParams(vmem_limit_bytes=VMEM_LIMIT),
        cost_estimate=pl.CostEstimate(flops=cost, bytes_accessed=1, transcendentals=0),
    )(*[value for value, _ in inputs], *flat, *after)
    return results[:-1], results[-1]


def label_kernel(sources, tokens_ref, ids_ref, weights_ref, out_ref):
    rows, width = tokens_ref.shape
    out_ref[:, :width] = tokens_ref[...]
    place = lax.broadcasted_iota(jnp.int32, (LANES, rows), 0)
    weight = jnp.zeros((LANES, rows), jnp.float32)
    for k in range(ids_ref.shape[0]):
        weight += jnp.where(ids_ref[k : k + 1, :] == place % sources, weights_ref[k : k + 1, :], 0.0)
    high = weight.astype(jnp.bfloat16).astype(jnp.float32)
    mid = (weight - high).astype(jnp.bfloat16).astype(jnp.float32)
    low = weight - high - mid
    term = place // sources
    picked = jnp.where(term == 0, high, jnp.where(term == 1, mid, jnp.where(term == 2, low, 0.0)))
    out_ref[:, width:] = jnp.transpose(picked).astype(jnp.bfloat16)


def collect(piece_refs, width, chunk_ref):
    start = 0
    for piece in piece_refs:
        chunk_ref[start : start + piece.shape[0], :] = piece[:, :width]
        start += piece.shape[0]


def partial_kernel(pieces, riders, tile, *refs):
    gate_ref, up_ref, *rider_refs, out_ref, chunk_ref = refs[pieces:]
    rows, width = chunk_ref.shape
    half = out_ref.shape[1]
    column = (1 - lax.axis_index("dp")) * half
    collect(refs[:pieces], width, chunk_ref)
    start = 2 * rows
    for ref in rider_refs:
        out_ref[start : start + ref.shape[0], :] = ref[...]
        start += ref.shape[0]

    @pl.loop(0, half // tile)
    def _(n):
        here = pl.ds(pl.multiple_of(column + n * tile, LANES), tile)
        there = pl.ds(pl.multiple_of(n * tile, LANES), tile)
        for i, ref in enumerate((gate_ref, up_ref)):
            part = jnp.dot(chunk_ref[...], ref[0, :, here], preferred_element_type=jnp.float32)
            out_ref[i * rows : (i + 1) * rows, there] = part.astype(jnp.bfloat16)


def hidden_kernel(pieces, tile, *refs):
    gate_ref, up_ref, arrived_ref, out_ref, chunk_ref = refs[pieces:]
    rows, width = chunk_ref.shape
    half = out_ref.shape[1]
    column = lax.axis_index("dp") * half
    collect(refs[:pieces], width, chunk_ref)

    @pl.loop(0, half // tile)
    def _(n):
        here = pl.ds(pl.multiple_of(column + n * tile, LANES), tile)
        there = pl.ds(pl.multiple_of(n * tile, LANES), tile)
        gate_sum, up_sum = (
            jnp.dot(chunk_ref[...], ref[0, :, here], preferred_element_type=jnp.float32)
            + arrived_ref[i * rows : (i + 1) * rows, there].astype(jnp.float32)
            for i, ref in enumerate((gate_ref, up_ref))
        )
        out_ref[:, there] = (gate_sum / (1.0 + jnp.exp(-gate_sum)) * up_sum).astype(jnp.bfloat16)


def output_kernel(pieces, sources, tile, behind, *refs):
    mine_ref, other_ref, down_ref = refs[pieces : pieces + 3]
    *out_refs, weight_ref = refs[pieces + 3 :]
    start = 0
    for piece in refs[:pieces]:
        rows = piece.shape[0]
        lane = lax.broadcasted_iota(jnp.int32, (rows, LANES), 1)
        label = piece[:, piece.shape[1] - LANES :].astype(jnp.float32)
        terms = jnp.where(lane % sources == lax.axis_index("expert"), label, 0.0)
        weight_ref[start : start + rows, :] = jnp.sum(terms, axis=1, keepdims=True)
        start += rows
    count, half = mine_ref.shape
    other = other_ref[behind : behind + count, :]
    first = lax.axis_index("dp") * half
    mine_rows = pl.ds(pl.multiple_of(first, LANES), half)
    other_rows = pl.ds(pl.multiple_of(half - first, LANES), half)

    @pl.loop(0, down_ref.shape[2] // tile)
    def _(n):
        here = pl.ds(pl.multiple_of(n * tile, LANES), tile)
        out = jnp.dot(mine_ref[...], down_ref[0, mine_rows, here], preferred_element_type=jnp.float32)
        out += jnp.dot(other, down_ref[0, other_rows, here], preferred_element_type=jnp.float32)
        out *= weight_ref[...]
        start = 0
        for ref in out_refs:
            ref[:, here] = out[start : start + ref.shape[0]].astype(ref.dtype)
            start += ref.shape[0]


def add_kernel(sums, *refs):
    inputs = 1 + max(i for terms in sums for i, _ in terms)
    for terms, out_ref in zip(sums, refs[inputs:], strict=True):
        rows = out_ref.shape[0]
        total = None
        for i, start in terms:
            value = refs[i][start : start + rows, :].astype(jnp.float32)
            total = value if total is None else total + value
        out_ref[...] = total.astype(out_ref.dtype)


def gather_body(tokens, expert_ids, gate_weights, gate_proj, up_proj, down_proj):
    rows, width = tokens.shape
    sources = lax.axis_size("expert")
    half = gate_proj.shape[2] // 2
    tile = 256 if half % 256 == 0 else half
    out_tile = 512 if width % 512 == 0 else width

    def swap(value, r):
        return lax.ppermute(value, "expert", [(i, i ^ r) for i in range(sources)])

    def cross(value):
        return lax.ppermute(value, "dp", [(0, 1), (1, 0)])

    def array(shape, dtype=jnp.bfloat16):
        return jax.ShapeDtypeStruct(shape, dtype)

    tail, number = [jnp.zeros(TOKEN.shape, TOKEN.dtype)], [0]

    def step(kernel, inputs, outputs, scratch=(), relays=()):
        results, token = call(
            kernel, inputs, outputs, list(tail), scratch, relays, COSTS.get(number[0], COST)
        )
        tail[:] = [token]
        number[0] += 1
        return results

    def count(pieces):
        return sum(p.shape[0] for p in pieces)

    def partials(pieces, riders=(), relays=()):
        total = count(pieces)
        sent, *relayed = step(
            functools.partial(partial_kernel, len(pieces), len(riders), tile),
            [*pieces, gate_proj, up_proj, *riders],
            [array((2 * total + count(riders), half))],
            [pltpu.VMEM((total, width), jnp.bfloat16)],
            relays,
        )
        return sent, *relayed

    def hidden(pieces, arrived, relays=()):
        total = count(pieces)
        mine, *relayed = step(
            functools.partial(hidden_kernel, len(pieces), tile),
            [*pieces, gate_proj, up_proj, arrived],
            [array((total, half))],
            [pltpu.VMEM((total, width), jnp.bfloat16)],
            relays,
        )
        return mine, *relayed

    def outputs(pieces, mine, arrived, behind, even, relays=()):
        total = count(pieces)
        made = [array((even, width), jnp.float32)] if even else []
        made += [array((total - even, width))] if total > even else []
        results = step(
            functools.partial(output_kernel, len(pieces), sources, out_tile, behind),
            [*pieces, mine, arrived, down_proj],
            made,
            [pltpu.VMEM((total, 1), jnp.float32)],
            relays,
        )
        kept = results[0] if even else None
        back = swap(results[len(made) - 1], 1) if total > even else None
        return kept, back, *results[len(made) :]

    def add(values, *sums, relays=()):
        return step(
            functools.partial(add_kernel, [terms for terms, _ in sums]),
            values,
            [shape for _, shape in sums],
            relays=relays,
        )

    def relay(*groups):
        return step(None, [], [], relays=[list(g) for g in groups])

    one, two, wide = array((rows, width)), array((2 * rows, width)), array((rows, width), jnp.float32)
    whole = [(0, 0), (1, 0)]

    def gap():
        step(None, [], [])

    def meet():
        tail.append(swap(tail[0], 1))

    (labelled,) = step(
        functools.partial(label_kernel, sources),
        [tokens, expert_ids.T, gate_weights.T],
        [array((rows, width + LANES))],
    )
    b1, z4 = swap(labelled, 1), swap(labelled, 4)
    p0 = [labelled, b1]
    (sent,) = partials(p0)
    y0 = cross(sent)
    (again,) = relay([labelled])
    z8 = swap(again, 8)
    meet()
    (b4,) = relay([z4])
    b5, x6 = swap(b4, 1), swap(b4, 2)
    gap()
    p1 = [b4, b5]
    (sent,) = partials(p1)
    y1 = cross(sent)
    (b6,) = relay([x6])
    b7 = swap(b6, 1)
    (h0,) = hidden(p0, y0)
    p2 = [b6, b7]
    (sent,) = partials(p2, [h0])
    y2 = cross(sent)
    b8, again = relay([z8], [again])
    x10, z12 = swap(b8, 2), swap(again, 12)
    (h1,) = hidden(p1, y1)
    (b8,) = relay([b8, x10])
    b9 = swap(b8, 1)
    gap()
    p3 = [b8, b9]
    (sent,) = partials(p3, [h1])
    y3 = cross(sent)
    (again,) = relay([again])
    x2 = swap(again, 2)
    meet()
    (h2,) = hidden(p2, y2)
    c0, c1 = outputs(p0, h0, y2, 4 * rows, rows)
    (b12,) = relay([z12])
    x14 = swap(b12, 2)
    (total,) = add([c0, c1], (whole, wide))
    (b12,) = relay([b12, x14])
    b13 = swap(b12, 1)
    gap()
    p4 = [b12, b13]
    (sent,) = partials(p4, [h2])
    y4 = cross(sent)
    (b2,) = relay([x2])
    b3 = swap(b2, 1)
    (h3,) = hidden(p3, y3)
    t3 = cross(h3)
    c4, c5 = outputs(p1, h1, y3, 8 * rows, rows)
    gap()
    (sent,) = add([c4, c5], (whole, one))
    s4 = swap(sent, 4)
    p5 = [b2, b3]
    (later,) = partials(p5)
    (h4,) = hidden(p4, y4)
    t4 = cross(h4)
    total, sent = add([total, s4], (whole, wide), relays=[[later]])
    y5 = cross(sent)
    c6, c7 = outputs(p2, h2, y4, 8 * rows, rows)
    gap()
    (sent,) = add([c6, c7], (whole, one))
    s6 = swap(sent, 6)
    c8, c9 = outputs(p3, h3, t3, 0, 2 * rows)
    gap()
    kept8, sent = add([c8, c9], (whole, wide), ([(0, rows), (1, rows)], one))
    x10 = swap(sent, 2)
    c12, c13 = outputs(p4, h4, t4, 0, 2 * rows)
    (total,) = add([total, s6], (whole, wide))
    kept12, sent = add([c12, c13], (whole, wide), ([(0, rows), (1, rows)], one))
    x14 = swap(sent, 2)
    (sent,) = add([kept8, x10], (whole, one))
    s8 = swap(sent, 8)
    (h5,) = hidden(p5, y5)
    t5 = cross(h5)
    (sent,) = add([kept12, x14], (whole, one))
    s12 = swap(sent, 12)
    c2, c3 = outputs(p5, h5, t5, 0, rows)
    gap()
    (sent,) = add([c2, c3], (whole, one))
    s2 = swap(sent, 2)
    (total,) = add([total, s8], (whole, wide))
    (total,) = add([total, s12, s2], (whole + [(2, 0)], one))
    return total


def solution(mesh):
    placed = (
        P("expert", "dp"),
        P("expert", None),
        P("expert", None),
        P("expert", "dp", None),
        P("expert", "dp", None),
        P("expert", None, "dp"),
    )

    def body(tokens, expert_ids, gate_weights, gate_proj, up_proj, down_proj):
        tok_count, top_count = expert_ids.shape
        sources = lax.axis_size("expert")
        whole_blocks = 2 * tok_count * top_count >= sources * tok_count
        paired = lax.axis_size("dp") == 2 and sources == 16
        plan = gather_body if whole_blocks and paired else dispatch_body
        return plan(tokens, expert_ids, gate_weights, gate_proj, up_proj, down_proj)

    return jax.shard_map(
        body, mesh=mesh, in_specs=placed, out_specs=P("expert", "dp"), check_vma=False
    )
```

```python
import functools

import jax
import jax.numpy as jnp
from jax import lax
from jax.experimental import pallas as pl
from jax.experimental.pallas import tpu as pltpu
from jax.sharding import PartitionSpec as P


def block_places(block_ids, expert_count, capacity):
    tok_count, top_count = block_ids.shape
    flat_ids = block_ids.reshape(tok_count * top_count)
    matches = (flat_ids[:, None] == jnp.arange(expert_count, dtype=jnp.int32)[None, :]).astype(
        jnp.int32
    )
    earlier = jnp.cumsum(matches, axis=0) - matches
    slot_index = jnp.sum(earlier * matches, axis=1)
    return (flat_ids * capacity + slot_index).reshape(tok_count, top_count)


def dispatch_body(tokens, expert_ids, gate_weights, gate_proj, up_proj, down_proj):
    tok_count, top_count = expert_ids.shape
    row_width = tokens.shape[1]
    sources = lax.axis_size("expert")
    capacity = 2 * tok_count * top_count // sources
    positions = jnp.arange(sources * capacity, dtype=jnp.int32)
    places = block_places(expert_ids, sources, capacity)
    matches = places[:, :, None] == positions[None, None, :]
    weighting = jnp.sum(jnp.where(matches, gate_weights[:, :, None], 0.0), axis=1)
    chosen = jnp.any(matches, axis=1).astype(jnp.bfloat16)
    outgoing = lax.dot_general(
        chosen, tokens, (((0,), (0,)), ((), ())), preferred_element_type=jnp.float32
    ).astype(jnp.bfloat16)
    incoming = lax.all_to_all(
        outgoing.reshape(sources, capacity, row_width),
        "expert",
        split_axis=0,
        concat_axis=0,
        tiled=True,
    )
    expert_rows = incoming.reshape(sources * capacity, row_width)
    gate_part = jnp.dot(expert_rows, gate_proj[0], preferred_element_type=jnp.float32)
    up_part = jnp.dot(expert_rows, up_proj[0], preferred_element_type=jnp.float32)
    gate_sum, up_sum = (
        lax.psum(gate_part.astype(jnp.bfloat16), "dp").astype(jnp.float32),
        lax.psum(up_part.astype(jnp.bfloat16), "dp").astype(jnp.float32),
    )
    hidden = (jax.nn.silu(gate_sum) * up_sum).astype(jnp.bfloat16)
    expert_out = jnp.dot(hidden, down_proj[0], preferred_element_type=jnp.float32).astype(
        jnp.bfloat16
    )
    returned = lax.all_to_all(
        expert_out.reshape(sources, capacity, row_width),
        "expert",
        split_axis=0,
        concat_axis=0,
        tiled=True,
    )
    returned_flat = returned.reshape(sources * capacity, row_width)
    weight_high = weighting.astype(jnp.bfloat16)
    weight_low = (weighting - weight_high.astype(jnp.float32)).astype(jnp.bfloat16)
    combined = jnp.dot(weight_high, returned_flat, preferred_element_type=jnp.float32)
    combined = combined + jnp.dot(weight_low, returned_flat, preferred_element_type=jnp.float32)
    return combined.astype(jnp.bfloat16)


LANES = 128
VMEM_LIMIT = 10 * 1024 * 1024
TOKEN = jax.ShapeDtypeStruct((8, LANES), jnp.float32)
HERE = pl.BlockSpec(memory_space=pltpu.VMEM)


def call(kernel, inputs, outputs, after, scratch=(), relays=()):
    inputs = [v if isinstance(v, tuple) else (v, HERE) for v in inputs]
    flat = [value for group in relays for value in group]
    joined = [
        jax.ShapeDtypeStruct((sum(v.shape[0] for v in group),) + group[0].shape[1:], group[0].dtype)
        for group in relays
    ]

    def run(*refs):
        refs = list(refs)
        taken = [refs.pop(0) for _ in inputs]
        carried = [refs.pop(0) for _ in flat]
        del refs[: len(after)]
        made = [refs.pop(0) for _ in outputs]
        joined_refs = [refs.pop(0) for _ in joined]
        token_ref = refs.pop(0)
        token_ref[...] = jnp.zeros(token_ref.shape, token_ref.dtype)
        for group, out_ref in zip(relays, joined_refs, strict=True):
            start = 0
            for _ in group:
                piece = carried.pop(0)
                out_ref[start : start + piece.shape[0], :] = piece[...]
                start += piece.shape[0]
        if kernel is not None:
            kernel(*taken, *made, *refs)

    results = pl.pallas_call(
        run,
        in_specs=[spec for _, spec in inputs] + [HERE] * len(flat) + [pl.BlockSpec(memory_space=pl.ANY)] * len(after),
        out_specs=[HERE] * (len(outputs) + len(joined) + 1),
        out_shape=list(outputs) + joined + [TOKEN],
        scratch_shapes=list(scratch),
        compiler_params=pltpu.CompilerParams(vmem_limit_bytes=VMEM_LIMIT),
        cost_estimate=pl.CostEstimate(flops=8_000_000_000, bytes_accessed=1, transcendentals=0),
    )(*[value for value, _ in inputs], *flat, *after)
    return results[:-1], results[-1]


def label_kernel(sources, tokens_ref, ids_ref, weights_ref, out_ref):
    rows, width = tokens_ref.shape
    out_ref[:, :width] = tokens_ref[...]
    place = lax.broadcasted_iota(jnp.int32, (LANES, rows), 0)
    weight = jnp.zeros((LANES, rows), jnp.float32)
    for k in range(ids_ref.shape[0]):
        weight += jnp.where(ids_ref[k : k + 1, :] == place % sources, weights_ref[k : k + 1, :], 0.0)
    high = weight.astype(jnp.bfloat16).astype(jnp.float32)
    mid = (weight - high).astype(jnp.bfloat16).astype(jnp.float32)
    low = weight - high - mid
    term = place // sources
    picked = jnp.where(term == 0, high, jnp.where(term == 1, mid, jnp.where(term == 2, low, 0.0)))
    out_ref[:, width:] = jnp.transpose(picked).astype(jnp.bfloat16)


def collect(piece_refs, width, chunk_ref):
    start = 0
    for piece in piece_refs:
        chunk_ref[start : start + piece.shape[0], :] = piece[:, :width]
        start += piece.shape[0]


def partial_kernel(pieces, riders, tile, *refs):
    gate_ref, up_ref, *rider_refs, out_ref, chunk_ref = refs[pieces:]
    rows, width = chunk_ref.shape
    half = out_ref.shape[1]
    column = (1 - lax.axis_index("dp")) * half
    collect(refs[:pieces], width, chunk_ref)
    start = 2 * rows
    for ref in rider_refs:
        out_ref[start : start + ref.shape[0], :] = ref[...]
        start += ref.shape[0]

    @pl.loop(0, half // tile)
    def _(n):
        here = pl.ds(pl.multiple_of(column + n * tile, LANES), tile)
        there = pl.ds(pl.multiple_of(n * tile, LANES), tile)
        for i, ref in enumerate((gate_ref, up_ref)):
            part = jnp.dot(chunk_ref[...], ref[0, :, here], preferred_element_type=jnp.float32)
            out_ref[i * rows : (i + 1) * rows, there] = part.astype(jnp.bfloat16)


def hidden_kernel(pieces, tile, *refs):
    gate_ref, up_ref, arrived_ref, out_ref, chunk_ref = refs[pieces:]
    rows, width = chunk_ref.shape
    half = out_ref.shape[1]
    column = lax.axis_index("dp") * half
    collect(refs[:pieces], width, chunk_ref)

    @pl.loop(0, half // tile)
    def _(n):
        here = pl.ds(pl.multiple_of(column + n * tile, LANES), tile)
        there = pl.ds(pl.multiple_of(n * tile, LANES), tile)
        gate_sum, up_sum = (
            jnp.dot(chunk_ref[...], ref[0, :, here], preferred_element_type=jnp.float32)
            + arrived_ref[i * rows : (i + 1) * rows, there].astype(jnp.float32)
            for i, ref in enumerate((gate_ref, up_ref))
        )
        out_ref[:, there] = (gate_sum / (1.0 + jnp.exp(-gate_sum)) * up_sum).astype(jnp.bfloat16)


def output_kernel(pieces, sources, tile, behind, *refs):
    mine_ref, other_ref, down_ref = refs[pieces : pieces + 3]
    *out_refs, weight_ref = refs[pieces + 3 :]
    start = 0
    for piece in refs[:pieces]:
        rows = piece.shape[0]
        lane = lax.broadcasted_iota(jnp.int32, (rows, LANES), 1)
        label = piece[:, piece.shape[1] - LANES :].astype(jnp.float32)
        terms = jnp.where(lane % sources == lax.axis_index("expert"), label, 0.0)
        weight_ref[start : start + rows, :] = jnp.sum(terms, axis=1, keepdims=True)
        start += rows
    count, half = mine_ref.shape
    other = other_ref[behind : behind + count, :]
    first = lax.axis_index("dp") * half
    mine_rows = pl.ds(pl.multiple_of(first, LANES), half)
    other_rows = pl.ds(pl.multiple_of(half - first, LANES), half)

    @pl.loop(0, down_ref.shape[2] // tile)
    def _(n):
        here = pl.ds(pl.multiple_of(n * tile, LANES), tile)
        out = jnp.dot(mine_ref[...], down_ref[0, mine_rows, here], preferred_element_type=jnp.float32)
        out += jnp.dot(other, down_ref[0, other_rows, here], preferred_element_type=jnp.float32)
        out *= weight_ref[...]
        start = 0
        for ref in out_refs:
            ref[:, here] = out[start : start + ref.shape[0]].astype(ref.dtype)
            start += ref.shape[0]


def add_kernel(sums, *refs):
    inputs = 1 + max(i for terms in sums for i, _ in terms)
    for terms, out_ref in zip(sums, refs[inputs:], strict=True):
        rows = out_ref.shape[0]
        total = None
        for i, start in terms:
            value = refs[i][start : start + rows, :].astype(jnp.float32)
            total = value if total is None else total + value
        out_ref[...] = total.astype(out_ref.dtype)


def gather_body(tokens, expert_ids, gate_weights, gate_proj, up_proj, down_proj):
    rows, width = tokens.shape
    sources = lax.axis_size("expert")
    half = gate_proj.shape[2] // 2
    tile = 256 if half % 256 == 0 else half
    out_tile = 512 if width % 512 == 0 else width

    def swap(value, r):
        return lax.ppermute(value, "expert", [(i, i ^ r) for i in range(sources)])

    def cross(value):
        return lax.ppermute(value, "dp", [(0, 1), (1, 0)])

    def array(shape, dtype=jnp.bfloat16):
        return jax.ShapeDtypeStruct(shape, dtype)

    tail = [jnp.zeros(TOKEN.shape, TOKEN.dtype)]

    def step(kernel, inputs, outputs, scratch=(), relays=()):
        results, token = call(
            kernel, inputs, outputs, list(tail), scratch, relays
        )
        tail[:] = [token]
        return results

    def count(pieces):
        return sum(p.shape[0] for p in pieces)

    def partials(pieces, riders=(), relays=()):
        total = count(pieces)
        sent, *relayed = step(
            functools.partial(partial_kernel, len(pieces), len(riders), tile),
            [*pieces, gate_proj, up_proj, *riders],
            [array((2 * total + count(riders), half))],
            [pltpu.VMEM((total, width), jnp.bfloat16)],
            relays,
        )
        return sent, *relayed

    def hidden(pieces, arrived, relays=()):
        total = count(pieces)
        mine, *relayed = step(
            functools.partial(hidden_kernel, len(pieces), tile),
            [*pieces, gate_proj, up_proj, arrived],
            [array((total, half))],
            [pltpu.VMEM((total, width), jnp.bfloat16)],
            relays,
        )
        return mine, *relayed

    def outputs(pieces, mine, arrived, behind, even, relays=()):
        total = count(pieces)
        made = [array((even, width), jnp.float32)] if even else []
        made += [array((total - even, width))] if total > even else []
        results = step(
            functools.partial(output_kernel, len(pieces), sources, out_tile, behind),
            [*pieces, mine, arrived, down_proj],
            made,
            [pltpu.VMEM((total, 1), jnp.float32)],
            relays,
        )
        kept = results[0] if even else None
        back = swap(results[len(made) - 1], 1) if total > even else None
        return kept, back, *results[len(made) :]

    def add(values, *sums, relays=()):
        return step(
            functools.partial(add_kernel, [terms for terms, _ in sums]),
            values,
            [shape for _, shape in sums],
            relays=relays,
        )

    def relay(*groups):
        return step(None, [], [], relays=[list(g) for g in groups])

    one, two, wide = array((rows, width)), array((2 * rows, width)), array((rows, width), jnp.float32)
    whole = [(0, 0), (1, 0)]

    def gap():
        step(None, [], [])

    def meet():
        tail.append(swap(tail[0], 1))

    (labelled,) = step(
        functools.partial(label_kernel, sources),
        [tokens, expert_ids.T, gate_weights.T],
        [array((rows, width + LANES))],
    )
    b1, z4 = swap(labelled, 1), swap(labelled, 4)
    p0 = [labelled, b1]
    (again,) = relay([labelled])
    z8 = swap(again, 8)
    (sent,) = partials(p0)
    y0 = cross(sent)
    meet()
    (b4,) = relay([z4])
    b5, x6 = swap(b4, 1), swap(b4, 2)
    gap()
    gap()
    p1 = [b4, b5]
    (sent,) = partials(p1)
    y1 = cross(sent)
    (b6,) = relay([x6])
    b7 = swap(b6, 1)
    (h0,) = hidden(p0, y0)
    (b8,) = relay([z8])
    x10 = swap(b8, 2)
    p2 = [b6, b7]
    (sent,) = partials(p2, [h0])
    y2 = cross(sent)
    (again,) = relay([labelled])
    z12 = swap(again, 12)
    (again,) = relay([labelled])
    x2 = swap(again, 2)
    (b8,) = relay([b8, x10])
    b9 = swap(b8, 1)
    (h1,) = hidden(p1, y1)
    gap()
    p3 = [b8, b9]
    (sent,) = partials(p3, [h1])
    y3 = cross(sent)
    meet()
    (h2,) = hidden(p2, y2)
    c0, c1 = outputs(p0, h0, y2, 4 * rows, rows)
    (b12,) = relay([z12])
    x14 = swap(b12, 2)
    (total,) = add([c0, c1], (whole, wide))
    (b12,) = relay([b12, x14])
    b13 = swap(b12, 1)
    gap()
    p4 = [b12, b13]
    (sent,) = partials(p4, [h2])
    y4 = cross(sent)
    (b2,) = relay([x2])
    b3 = swap(b2, 1)
    (h3,) = hidden(p3, y3)
    t3 = cross(h3)
    c4, c5 = outputs(p1, h1, y3, 8 * rows, rows)
    gap()
    (sent,) = add([c4, c5], (whole, one))
    s4 = swap(sent, 4)
    p5 = [b2, b3]
    (later,) = partials(p5)
    (h4,) = hidden(p4, y4)
    t4 = cross(h4)
    (later,) = relay([later])
    y5 = cross(later)
    c6, c7 = outputs(p2, h2, y4, 8 * rows, rows)
    gap()
    (total,) = add([total, s4], (whole, wide))
    gap()
    (sent,) = add([c6, c7], (whole, one))
    s6 = swap(sent, 6)
    c8, c9 = outputs(p3, h3, t3, 0, 2 * rows)
    gap()
    kept8, sent = add([c8, c9], (whole, wide), ([(0, rows), (1, rows)], one))
    x10 = swap(sent, 2)
    c12, c13 = outputs(p4, h4, t4, 0, 2 * rows)
    note = swap(tail[0], 1)
    (total,) = add([total, s6], (whole, wide))
    kept12, sent = add([c12, c13], (whole, wide), ([(0, rows), (1, rows)], one))
    x14 = swap(sent, 2)
    (sent,) = add([kept8, x10], (whole, one))
    s8 = swap(sent, 8)
    (h5,) = hidden(p5, y5)
    t5 = cross(h5)
    (sent,) = add([kept12, x14], (whole, one))
    s12 = swap(sent, 12)
    tail.append(note)
    c2, c3 = outputs(p5, h5, t5, 0, rows)
    gap()
    (sent,) = add([c2, c3], (whole, one))
    s2 = swap(sent, 2)
    (total,) = add([total, s8], (whole, wide))
    (total,) = add([total, s12, s2], (whole + [(2, 0)], one))
    return total


def solution(mesh):
    placed = (
        P("expert", "dp"),
        P("expert", None),
        P("expert", None),
        P("expert", "dp", None),
        P("expert", "dp", None),
        P("expert", None, "dp"),
    )

    def body(tokens, expert_ids, gate_weights, gate_proj, up_proj, down_proj):
        tok_count, top_count = expert_ids.shape
        sources = lax.axis_size("expert")
        whole_blocks = 2 * tok_count * top_count >= sources * tok_count
        paired = lax.axis_size("dp") == 2 and sources == 16
        plan = gather_body if whole_blocks and paired else dispatch_body
        return plan(tokens, expert_ids, gate_weights, gate_proj, up_proj, down_proj)

    return jax.shard_map(
        body, mesh=mesh, in_specs=placed, out_specs=P("expert", "dp"), check_vma=False
    )
```

```python
import functools

import jax
import jax.numpy as jnp
from jax import lax
from jax.experimental import pallas as pl
from jax.experimental.pallas import tpu as pltpu
from jax.sharding import PartitionSpec as P


def block_places(block_ids, expert_count, capacity):
    tok_count, top_count = block_ids.shape
    flat_ids = block_ids.reshape(tok_count * top_count)
    matches = (flat_ids[:, None] == jnp.arange(expert_count, dtype=jnp.int32)[None, :]).astype(
        jnp.int32
    )
    earlier = jnp.cumsum(matches, axis=0) - matches
    slot_index = jnp.sum(earlier * matches, axis=1)
    return (flat_ids * capacity + slot_index).reshape(tok_count, top_count)


def dispatch_body(tokens, expert_ids, gate_weights, gate_proj, up_proj, down_proj):
    tok_count, top_count = expert_ids.shape
    row_width = tokens.shape[1]
    sources = lax.axis_size("expert")
    capacity = 2 * tok_count * top_count // sources
    positions = jnp.arange(sources * capacity, dtype=jnp.int32)
    places = block_places(expert_ids, sources, capacity)
    matches = places[:, :, None] == positions[None, None, :]
    weighting = jnp.sum(jnp.where(matches, gate_weights[:, :, None], 0.0), axis=1)
    chosen = jnp.any(matches, axis=1).astype(jnp.bfloat16)
    outgoing = lax.dot_general(
        chosen, tokens, (((0,), (0,)), ((), ())), preferred_element_type=jnp.float32
    ).astype(jnp.bfloat16)
    incoming = lax.all_to_all(
        outgoing.reshape(sources, capacity, row_width),
        "expert",
        split_axis=0,
        concat_axis=0,
        tiled=True,
    )
    expert_rows = incoming.reshape(sources * capacity, row_width)
    gate_part = jnp.dot(expert_rows, gate_proj[0], preferred_element_type=jnp.float32)
    up_part = jnp.dot(expert_rows, up_proj[0], preferred_element_type=jnp.float32)
    gate_sum, up_sum = (
        lax.psum(gate_part.astype(jnp.bfloat16), "dp").astype(jnp.float32),
        lax.psum(up_part.astype(jnp.bfloat16), "dp").astype(jnp.float32),
    )
    hidden = (jax.nn.silu(gate_sum) * up_sum).astype(jnp.bfloat16)
    expert_out = jnp.dot(hidden, down_proj[0], preferred_element_type=jnp.float32).astype(
        jnp.bfloat16
    )
    returned = lax.all_to_all(
        expert_out.reshape(sources, capacity, row_width),
        "expert",
        split_axis=0,
        concat_axis=0,
        tiled=True,
    )
    returned_flat = returned.reshape(sources * capacity, row_width)
    weight_high = weighting.astype(jnp.bfloat16)
    weight_low = (weighting - weight_high.astype(jnp.float32)).astype(jnp.bfloat16)
    combined = jnp.dot(weight_high, returned_flat, preferred_element_type=jnp.float32)
    combined = combined + jnp.dot(weight_low, returned_flat, preferred_element_type=jnp.float32)
    return combined.astype(jnp.bfloat16)


LANES = 128
VMEM_LIMIT = 10 * 1024 * 1024
COST = 8_000_000_000
TOKEN = jax.ShapeDtypeStruct((8, LANES), jnp.float32)
HERE = pl.BlockSpec(memory_space=pltpu.VMEM)


def call(kernel, inputs, outputs, after, scratch=(), relays=(), cost=0):
    inputs = [v if isinstance(v, tuple) else (v, HERE) for v in inputs]
    flat = [value for group in relays for value in group]
    joined = [
        jax.ShapeDtypeStruct((sum(v.shape[0] for v in group),) + group[0].shape[1:], group[0].dtype)
        for group in relays
    ]

    def run(*refs):
        refs = list(refs)
        taken = [refs.pop(0) for _ in inputs]
        carried = [refs.pop(0) for _ in flat]
        del refs[: len(after)]
        made = [refs.pop(0) for _ in outputs]
        joined_refs = [refs.pop(0) for _ in joined]
        token_ref = refs.pop(0)
        token_ref[...] = jnp.zeros(token_ref.shape, token_ref.dtype)
        for group, out_ref in zip(relays, joined_refs, strict=True):
            start = 0
            for _ in group:
                piece = carried.pop(0)
                out_ref[start : start + piece.shape[0], :] = piece[...]
                start += piece.shape[0]
        if kernel is not None:
            kernel(*taken, *made, *refs)

    results = pl.pallas_call(
        run,
        in_specs=[spec for _, spec in inputs] + [HERE] * len(flat) + [pl.BlockSpec(memory_space=pl.ANY)] * len(after),
        out_specs=[HERE] * (len(outputs) + len(joined) + 1),
        out_shape=list(outputs) + joined + [TOKEN],
        scratch_shapes=list(scratch),
        compiler_params=pltpu.CompilerParams(vmem_limit_bytes=VMEM_LIMIT),
        cost_estimate=pl.CostEstimate(flops=cost, bytes_accessed=1, transcendentals=0),
    )(*[value for value, _ in inputs], *flat, *after)
    return results[:-1], results[-1]


def label_kernel(sources, tokens_ref, ids_ref, weights_ref, out_ref):
    rows, width = tokens_ref.shape
    out_ref[:, :width] = tokens_ref[...]
    place = lax.broadcasted_iota(jnp.int32, (LANES, rows), 0)
    weight = jnp.zeros((LANES, rows), jnp.float32)
    for k in range(ids_ref.shape[0]):
        weight += jnp.where(ids_ref[k : k + 1, :] == place % sources, weights_ref[k : k + 1, :], 0.0)
    high = weight.astype(jnp.bfloat16).astype(jnp.float32)
    mid = (weight - high).astype(jnp.bfloat16).astype(jnp.float32)
    low = weight - high - mid
    term = place // sources
    picked = jnp.where(term == 0, high, jnp.where(term == 1, mid, jnp.where(term == 2, low, 0.0)))
    out_ref[:, width:] = jnp.transpose(picked).astype(jnp.bfloat16)


def collect(piece_refs, width, chunk_ref):
    start = 0
    for piece in piece_refs:
        chunk_ref[start : start + piece.shape[0], :] = piece[:, :width]
        start += piece.shape[0]


def partial_kernel(pieces, riders, tile, *refs):
    gate_ref, up_ref, *rider_refs, out_ref, chunk_ref = refs[pieces:]
    rows, width = chunk_ref.shape
    half = out_ref.shape[1]
    column = (1 - lax.axis_index("dp")) * half
    collect(refs[:pieces], width, chunk_ref)
    start = 2 * rows
    for ref in rider_refs:
        out_ref[start : start + ref.shape[0], :] = ref[...]
        start += ref.shape[0]

    @pl.loop(0, half // tile)
    def _(n):
        here = pl.ds(pl.multiple_of(column + n * tile, LANES), tile)
        there = pl.ds(pl.multiple_of(n * tile, LANES), tile)
        for i, ref in enumerate((gate_ref, up_ref)):
            part = jnp.dot(chunk_ref[...], ref[0, :, here], preferred_element_type=jnp.float32)
            out_ref[i * rows : (i + 1) * rows, there] = part.astype(jnp.bfloat16)


def hidden_kernel(pieces, tile, *refs):
    gate_ref, up_ref, arrived_ref, out_ref, chunk_ref = refs[pieces:]
    rows, width = chunk_ref.shape
    half = out_ref.shape[1]
    column = lax.axis_index("dp") * half
    collect(refs[:pieces], width, chunk_ref)

    @pl.loop(0, half // tile)
    def _(n):
        here = pl.ds(pl.multiple_of(column + n * tile, LANES), tile)
        there = pl.ds(pl.multiple_of(n * tile, LANES), tile)
        gate_sum, up_sum = (
            jnp.dot(chunk_ref[...], ref[0, :, here], preferred_element_type=jnp.float32)
            + arrived_ref[i * rows : (i + 1) * rows, there].astype(jnp.float32)
            for i, ref in enumerate((gate_ref, up_ref))
        )
        out_ref[:, there] = (gate_sum / (1.0 + jnp.exp(-gate_sum)) * up_sum).astype(jnp.bfloat16)


def output_kernel(pieces, sources, tile, behind, *refs):
    mine_ref, other_ref, down_ref = refs[pieces : pieces + 3]
    *out_refs, weight_ref = refs[pieces + 3 :]
    start = 0
    for piece in refs[:pieces]:
        rows = piece.shape[0]
        lane = lax.broadcasted_iota(jnp.int32, (rows, LANES), 1)
        label = piece[:, piece.shape[1] - LANES :].astype(jnp.float32)
        terms = jnp.where(lane % sources == lax.axis_index("expert"), label, 0.0)
        weight_ref[start : start + rows, :] = jnp.sum(terms, axis=1, keepdims=True)
        start += rows
    count, half = mine_ref.shape
    other = other_ref[behind : behind + count, :]
    first = lax.axis_index("dp") * half
    mine_rows = pl.ds(pl.multiple_of(first, LANES), half)
    other_rows = pl.ds(pl.multiple_of(half - first, LANES), half)

    @pl.loop(0, down_ref.shape[2] // tile)
    def _(n):
        here = pl.ds(pl.multiple_of(n * tile, LANES), tile)
        out = jnp.dot(mine_ref[...], down_ref[0, mine_rows, here], preferred_element_type=jnp.float32)
        out += jnp.dot(other, down_ref[0, other_rows, here], preferred_element_type=jnp.float32)
        out *= weight_ref[...]
        start = 0
        for ref in out_refs:
            ref[:, here] = out[start : start + ref.shape[0]].astype(ref.dtype)
            start += ref.shape[0]


def add_kernel(sums, *refs):
    inputs = 1 + max(i for terms in sums for i, _ in terms)
    for terms, out_ref in zip(sums, refs[inputs:], strict=True):
        rows = out_ref.shape[0]
        total = None
        for i, start in terms:
            value = refs[i][start : start + rows, :].astype(jnp.float32)
            total = value if total is None else total + value
        out_ref[...] = total.astype(out_ref.dtype)


def gather_body(tokens, expert_ids, gate_weights, gate_proj, up_proj, down_proj):
    rows, width = tokens.shape
    sources = lax.axis_size("expert")
    half = gate_proj.shape[2] // 2
    tile = 256 if half % 256 == 0 else half
    out_tile = 512 if width % 512 == 0 else width

    def swap(value, r):
        return lax.ppermute(value, "expert", [(i, i ^ r) for i in range(sources)])

    def cross(value):
        return lax.ppermute(value, "dp", [(0, 1), (1, 0)])

    def array(shape, dtype=jnp.bfloat16):
        return jax.ShapeDtypeStruct(shape, dtype)

    tail, cost = [jnp.zeros(TOKEN.shape, TOKEN.dtype)], [COST]

    def step(kernel, inputs, outputs, scratch=(), relays=()):
        results, token = call(
            kernel, inputs, outputs, list(tail), scratch, relays, cost[0]
        )
        tail[:] = [token]
        return results

    def count(pieces):
        return sum(p.shape[0] for p in pieces)

    def partials(pieces, riders=(), relays=()):
        total = count(pieces)
        sent, *relayed = step(
            functools.partial(partial_kernel, len(pieces), len(riders), tile),
            [*pieces, gate_proj, up_proj, *riders],
            [array((2 * total + count(riders), half))],
            [pltpu.VMEM((total, width), jnp.bfloat16)],
            relays,
        )
        return sent, *relayed

    def hidden(pieces, arrived, relays=()):
        total = count(pieces)
        mine, *relayed = step(
            functools.partial(hidden_kernel, len(pieces), tile),
            [*pieces, gate_proj, up_proj, arrived],
            [array((total, half))],
            [pltpu.VMEM((total, width), jnp.bfloat16)],
            relays,
        )
        return mine, *relayed

    def outputs(pieces, mine, arrived, behind, even, relays=()):
        total = count(pieces)
        made = [array((even, width), jnp.float32)] if even else []
        made += [array((total - even, width))] if total > even else []
        results = step(
            functools.partial(output_kernel, len(pieces), sources, out_tile, behind),
            [*pieces, mine, arrived, down_proj],
            made,
            [pltpu.VMEM((total, 1), jnp.float32)],
            relays,
        )
        kept = results[0] if even else None
        back = swap(results[len(made) - 1], 1) if total > even else None
        return kept, back, *results[len(made) :]

    def add(values, *sums, relays=()):
        return step(
            functools.partial(add_kernel, [terms for terms, _ in sums]),
            values,
            [shape for _, shape in sums],
            relays=relays,
        )

    def relay(*groups):
        return step(None, [], [], relays=[list(g) for g in groups])

    one, two, wide = array((rows, width)), array((2 * rows, width)), array((rows, width), jnp.float32)
    whole = [(0, 0), (1, 0)]

    def gap():
        step(None, [], [])

    def meet():
        tail.append(swap(tail[0], 1))

    (labelled,) = step(
        functools.partial(label_kernel, sources),
        [tokens, expert_ids.T, gate_weights.T],
        [array((rows, width + LANES))],
    )
    b1, z4 = swap(labelled, 1), swap(labelled, 4)
    p0 = [labelled, b1]
    (again,) = relay([labelled])
    z8 = swap(again, 8)
    (sent,) = partials(p0)
    y0 = cross(sent)
    cost[0] = 1
    meet()
    cost[0] = COST
    (b4,) = relay([z4])
    b5, x6 = swap(b4, 1), swap(b4, 2)
    gap()
    gap()
    p1 = [b4, b5]
    (sent,) = partials(p1)
    y1 = cross(sent)
    note3 = swap(tail[0], 1)
    (h0,) = hidden(p0, y0)
    tail.append(note3)
    (b6,) = relay([x6])
    b7 = swap(b6, 1)
    (b8,) = relay([z8])
    x10 = swap(b8, 2)
    p2 = [b6, b7]
    (sent,) = partials(p2, [h0])
    y2 = cross(sent)
    (h1,) = hidden(p1, y1)
    (again,) = relay([labelled])
    z12 = swap(again, 12)
    (b8,) = relay([b8, x10])
    b9 = swap(b8, 1)
    gap()
    p3 = [b8, b9]
    (sent,) = partials(p3, [h1])
    y3 = cross(sent)
    (again,) = relay([labelled])
    x2 = swap(again, 2)
    (h2,) = hidden(p2, y2)
    c0, c1 = outputs(p0, h0, y2, 4 * rows, rows)
    (b12,) = relay([z12])
    x14 = swap(b12, 2)
    (total,) = add([c0, c1], (whole, wide))
    (b12,) = relay([b12, x14])
    b13 = swap(b12, 1)
    gap()
    p4 = [b12, b13]
    (sent,) = partials(p4, [h2])
    y4 = cross(sent)
    (b2,) = relay([x2])
    b3 = swap(b2, 1)
    (h3,) = hidden(p3, y3)
    t3 = cross(h3)
    c4, c5 = outputs(p1, h1, y3, 8 * rows, rows)
    gap()
    (sent,) = add([c4, c5], (whole, one))
    s4 = swap(sent, 4)
    (latera,) = partials([b3])
    (later,) = partials([b2])
    (h4,) = hidden(p4, y4)
    t4 = cross(h4)
    (latera,) = relay([latera])
    y5a = cross(latera)
    (later,) = relay([later])
    y5 = cross(later)
    c6, c7 = outputs(p2, h2, y4, 8 * rows, rows)
    (total,) = add([total, s4], (whole, wide))
    gap()
    (sent,) = add([c6, c7], (whole, one))
    s6 = swap(sent, 6)
    c8, c9 = outputs(p3, h3, t3, 0, 2 * rows)
    gap()
    kept8, sent = add([c8, c9], (whole, wide), ([(0, rows), (1, rows)], one))
    x10 = swap(sent, 2)
    c12, c13 = outputs(p4, h4, t4, 0, 2 * rows)
    note2 = swap(tail[0], 1)
    (total,) = add([total, s6], (whole, wide))
    (h5a,) = hidden([b3], y5a)
    t5a = cross(h5a)
    kept12, sent = add([c12, c13], (whole, wide), ([(0, rows), (1, rows)], one))
    x14 = swap(sent, 2)
    (sent,) = add([kept8, x10], (whole, one))
    s8 = swap(sent, 8)
    _, c3 = outputs([b3], h5a, t5a, 0, 0)
    (h5,) = hidden([b2], y5)
    t5 = cross(h5)
    (sent,) = add([kept12, x14], (whole, one))
    s12 = swap(sent, 12)
    tail.append(note2)
    c2, _ = outputs([b2], h5, t5, 0, rows)
    gap()
    (sent,) = add([c2, c3], (whole, one))
    s2 = swap(sent, 2)
    (total,) = add([total, s8], (whole, wide))
    (total,) = add([total, s12, s2], (whole + [(2, 0)], one))
    return total


def solution(mesh):
    placed = (
        P("expert", "dp"),
        P("expert", None),
        P("expert", None),
        P("expert", "dp", None),
        P("expert", "dp", None),
        P("expert", None, "dp"),
    )

    def body(tokens, expert_ids, gate_weights, gate_proj, up_proj, down_proj):
        tok_count, top_count = expert_ids.shape
        sources = lax.axis_size("expert")
        whole_blocks = 2 * tok_count * top_count >= sources * tok_count
        paired = lax.axis_size("dp") == 2 and sources == 16
        plan = gather_body if whole_blocks and paired else dispatch_body
        return plan(tokens, expert_ids, gate_weights, gate_proj, up_proj, down_proj)

    return jax.shard_map(
        body, mesh=mesh, in_specs=placed, out_specs=P("expert", "dp"), check_vma=False
    )
```

```python
import functools

import jax
import jax.numpy as jnp
from jax import lax
from jax.experimental import pallas as pl
from jax.experimental.pallas import tpu as pltpu
from jax.sharding import PartitionSpec as P


def block_places(block_ids, expert_count, capacity):
    tok_count, top_count = block_ids.shape
    flat_ids = block_ids.reshape(tok_count * top_count)
    matches = (flat_ids[:, None] == jnp.arange(expert_count, dtype=jnp.int32)[None, :]).astype(
        jnp.int32
    )
    earlier = jnp.cumsum(matches, axis=0) - matches
    slot_index = jnp.sum(earlier * matches, axis=1)
    return (flat_ids * capacity + slot_index).reshape(tok_count, top_count)


def dispatch_body(tokens, expert_ids, gate_weights, gate_proj, up_proj, down_proj):
    tok_count, top_count = expert_ids.shape
    row_width = tokens.shape[1]
    sources = lax.axis_size("expert")
    capacity = 2 * tok_count * top_count // sources
    positions = jnp.arange(sources * capacity, dtype=jnp.int32)
    places = block_places(expert_ids, sources, capacity)
    matches = places[:, :, None] == positions[None, None, :]
    weighting = jnp.sum(jnp.where(matches, gate_weights[:, :, None], 0.0), axis=1)
    chosen = jnp.any(matches, axis=1).astype(jnp.bfloat16)
    outgoing = lax.dot_general(
        chosen, tokens, (((0,), (0,)), ((), ())), preferred_element_type=jnp.float32
    ).astype(jnp.bfloat16)
    incoming = lax.all_to_all(
        outgoing.reshape(sources, capacity, row_width),
        "expert",
        split_axis=0,
        concat_axis=0,
        tiled=True,
    )
    expert_rows = incoming.reshape(sources * capacity, row_width)
    gate_part = jnp.dot(expert_rows, gate_proj[0], preferred_element_type=jnp.float32)
    up_part = jnp.dot(expert_rows, up_proj[0], preferred_element_type=jnp.float32)
    gate_sum, up_sum = (
        lax.psum(gate_part.astype(jnp.bfloat16), "dp").astype(jnp.float32),
        lax.psum(up_part.astype(jnp.bfloat16), "dp").astype(jnp.float32),
    )
    hidden = (jax.nn.silu(gate_sum) * up_sum).astype(jnp.bfloat16)
    expert_out = jnp.dot(hidden, down_proj[0], preferred_element_type=jnp.float32).astype(
        jnp.bfloat16
    )
    returned = lax.all_to_all(
        expert_out.reshape(sources, capacity, row_width),
        "expert",
        split_axis=0,
        concat_axis=0,
        tiled=True,
    )
    returned_flat = returned.reshape(sources * capacity, row_width)
    weight_high = weighting.astype(jnp.bfloat16)
    weight_low = (weighting - weight_high.astype(jnp.float32)).astype(jnp.bfloat16)
    combined = jnp.dot(weight_high, returned_flat, preferred_element_type=jnp.float32)
    combined = combined + jnp.dot(weight_low, returned_flat, preferred_element_type=jnp.float32)
    return combined.astype(jnp.bfloat16)


LANES = 128
VMEM_LIMIT = 10 * 1024 * 1024
TOKEN = jax.ShapeDtypeStruct((8, LANES), jnp.float32)
HERE = pl.BlockSpec(memory_space=pltpu.VMEM)


def call(kernel, inputs, outputs, after, scratch=(), relays=()):
    inputs = [v if isinstance(v, tuple) else (v, HERE) for v in inputs]
    flat = [value for group in relays for value in group]
    joined = [
        jax.ShapeDtypeStruct((sum(v.shape[0] for v in group),) + group[0].shape[1:], group[0].dtype)
        for group in relays
    ]

    def run(*refs):
        refs = list(refs)
        taken = [refs.pop(0) for _ in inputs]
        carried = [refs.pop(0) for _ in flat]
        del refs[: len(after)]
        made = [refs.pop(0) for _ in outputs]
        joined_refs = [refs.pop(0) for _ in joined]
        token_ref = refs.pop(0)
        token_ref[...] = jnp.zeros(token_ref.shape, token_ref.dtype)
        for group, out_ref in zip(relays, joined_refs, strict=True):
            start = 0
            for _ in group:
                piece = carried.pop(0)
                out_ref[start : start + piece.shape[0], :] = piece[...]
                start += piece.shape[0]
        if kernel is not None:
            kernel(*taken, *made, *refs)

    results = pl.pallas_call(
        run,
        in_specs=[spec for _, spec in inputs] + [HERE] * len(flat) + [pl.BlockSpec(memory_space=pl.ANY)] * len(after),
        out_specs=[HERE] * (len(outputs) + len(joined) + 1),
        out_shape=list(outputs) + joined + [TOKEN],
        scratch_shapes=list(scratch),
        compiler_params=pltpu.CompilerParams(vmem_limit_bytes=VMEM_LIMIT),
        cost_estimate=pl.CostEstimate(flops=8_000_000_000, bytes_accessed=1, transcendentals=0),
    )(*[value for value, _ in inputs], *flat, *after)
    return results[:-1], results[-1]


def label_kernel(sources, tokens_ref, ids_ref, weights_ref, out_ref):
    rows, width = tokens_ref.shape
    out_ref[:, :width] = tokens_ref[...]
    place = lax.broadcasted_iota(jnp.int32, (LANES, rows), 0)
    weight = jnp.zeros((LANES, rows), jnp.float32)
    for k in range(ids_ref.shape[0]):
        weight += jnp.where(ids_ref[k : k + 1, :] == place % sources, weights_ref[k : k + 1, :], 0.0)
    high = weight.astype(jnp.bfloat16).astype(jnp.float32)
    mid = (weight - high).astype(jnp.bfloat16).astype(jnp.float32)
    low = weight - high - mid
    term = place // sources
    picked = jnp.where(term == 0, high, jnp.where(term == 1, mid, jnp.where(term == 2, low, 0.0)))
    out_ref[:, width:] = jnp.transpose(picked).astype(jnp.bfloat16)


def collect(piece_refs, width, chunk_ref):
    start = 0
    for piece in piece_refs:
        chunk_ref[start : start + piece.shape[0], :] = piece[:, :width]
        start += piece.shape[0]


def partial_kernel(pieces, riders, tile, *refs):
    gate_ref, up_ref, *rider_refs, out_ref, chunk_ref = refs[pieces:]
    rows, width = chunk_ref.shape
    half = out_ref.shape[1]
    column = (1 - lax.axis_index("dp")) * half
    collect(refs[:pieces], width, chunk_ref)
    start = 2 * rows
    for ref in rider_refs:
        out_ref[start : start + ref.shape[0], :] = ref[...]
        start += ref.shape[0]

    @pl.loop(0, half // tile)
    def _(n):
        here = pl.ds(pl.multiple_of(column + n * tile, LANES), tile)
        there = pl.ds(pl.multiple_of(n * tile, LANES), tile)
        for i, ref in enumerate((gate_ref, up_ref)):
            part = jnp.dot(chunk_ref[...], ref[0, :, here], preferred_element_type=jnp.float32)
            out_ref[i * rows : (i + 1) * rows, there] = part.astype(jnp.bfloat16)


def hidden_kernel(pieces, tile, *refs):
    gate_ref, up_ref, arrived_ref, out_ref, chunk_ref = refs[pieces:]
    rows, width = chunk_ref.shape
    half = out_ref.shape[1]
    column = lax.axis_index("dp") * half
    collect(refs[:pieces], width, chunk_ref)

    @pl.loop(0, half // tile)
    def _(n):
        here = pl.ds(pl.multiple_of(column + n * tile, LANES), tile)
        there = pl.ds(pl.multiple_of(n * tile, LANES), tile)
        gate_sum, up_sum = (
            jnp.dot(chunk_ref[...], ref[0, :, here], preferred_element_type=jnp.float32)
            + arrived_ref[i * rows : (i + 1) * rows, there].astype(jnp.float32)
            for i, ref in enumerate((gate_ref, up_ref))
        )
        out_ref[:, there] = (gate_sum / (1.0 + jnp.exp(-gate_sum)) * up_sum).astype(jnp.bfloat16)


def output_kernel(pieces, sources, tile, behind, *refs):
    mine_ref, other_ref, down_ref = refs[pieces : pieces + 3]
    *out_refs, weight_ref = refs[pieces + 3 :]
    start = 0
    for piece in refs[:pieces]:
        rows = piece.shape[0]
        lane = lax.broadcasted_iota(jnp.int32, (rows, LANES), 1)
        label = piece[:, piece.shape[1] - LANES :].astype(jnp.float32)
        terms = jnp.where(lane % sources == lax.axis_index("expert"), label, 0.0)
        weight_ref[start : start + rows, :] = jnp.sum(terms, axis=1, keepdims=True)
        start += rows
    count, half = mine_ref.shape
    other = other_ref[behind : behind + count, :]
    first = lax.axis_index("dp") * half
    mine_rows = pl.ds(pl.multiple_of(first, LANES), half)
    other_rows = pl.ds(pl.multiple_of(half - first, LANES), half)

    @pl.loop(0, down_ref.shape[2] // tile)
    def _(n):
        here = pl.ds(pl.multiple_of(n * tile, LANES), tile)
        out = jnp.dot(mine_ref[...], down_ref[0, mine_rows, here], preferred_element_type=jnp.float32)
        out += jnp.dot(other, down_ref[0, other_rows, here], preferred_element_type=jnp.float32)
        out *= weight_ref[...]
        start = 0
        for ref in out_refs:
            ref[:, here] = out[start : start + ref.shape[0]].astype(ref.dtype)
            start += ref.shape[0]


def add_kernel(sums, *refs):
    inputs = 1 + max(i for terms in sums for i, _ in terms)
    for terms, out_ref in zip(sums, refs[inputs:], strict=True):
        rows = out_ref.shape[0]
        total = None
        for i, start in terms:
            value = refs[i][start : start + rows, :].astype(jnp.float32)
            total = value if total is None else total + value
        out_ref[...] = total.astype(out_ref.dtype)


def gather_body(tokens, expert_ids, gate_weights, gate_proj, up_proj, down_proj):
    rows, width = tokens.shape
    sources = lax.axis_size("expert")
    half = gate_proj.shape[2] // 2
    tile = 256 if half % 256 == 0 else half
    out_tile = 512 if width % 512 == 0 else width

    def swap(value, r):
        return lax.ppermute(value, "expert", [(i, i ^ r) for i in range(sources)])

    def cross(value):
        return lax.ppermute(value, "dp", [(0, 1), (1, 0)])

    def array(shape, dtype=jnp.bfloat16):
        return jax.ShapeDtypeStruct(shape, dtype)

    tail = [jnp.zeros(TOKEN.shape, TOKEN.dtype)]

    def step(kernel, inputs, outputs, scratch=(), relays=()):
        results, token = call(kernel, inputs, outputs, list(tail), scratch, relays)
        tail[:] = [token]
        return results

    def count(pieces):
        return sum(p.shape[0] for p in pieces)

    def partials(pieces, riders=(), relays=()):
        total = count(pieces)
        sent, *relayed = step(
            functools.partial(partial_kernel, len(pieces), len(riders), tile),
            [*pieces, gate_proj, up_proj, *riders],
            [array((2 * total + count(riders), half))],
            [pltpu.VMEM((total, width), jnp.bfloat16)],
            relays,
        )
        return sent, *relayed

    def hidden(pieces, arrived, relays=()):
        total = count(pieces)
        mine, *relayed = step(
            functools.partial(hidden_kernel, len(pieces), tile),
            [*pieces, gate_proj, up_proj, arrived],
            [array((total, half))],
            [pltpu.VMEM((total, width), jnp.bfloat16)],
            relays,
        )
        return mine, *relayed

    def outputs(pieces, mine, arrived, behind, even, relays=()):
        total = count(pieces)
        made = [array((even, width), jnp.float32)] if even else []
        made += [array((total - even, width))] if total > even else []
        results = step(
            functools.partial(output_kernel, len(pieces), sources, out_tile, behind),
            [*pieces, mine, arrived, down_proj],
            made,
            [pltpu.VMEM((total, 1), jnp.float32)],
            relays,
        )
        kept = results[0] if even else None
        back = swap(results[len(made) - 1], 1) if total > even else None
        return kept, back, *results[len(made) :]

    def add(values, *sums, relays=()):
        return step(
            functools.partial(add_kernel, [terms for terms, _ in sums]),
            values,
            [shape for _, shape in sums],
            relays=relays,
        )

    def relay(*groups):
        return step(None, [], [], relays=[list(g) for g in groups])

    one, two, wide = array((rows, width)), array((2 * rows, width)), array((rows, width), jnp.float32)
    whole = [(0, 0), (1, 0)]

    def gap():
        step(None, [], [])

    def meet():
        tail.append(swap(tail[0], 1))

    (labelled,) = step(
        functools.partial(label_kernel, sources),
        [tokens, expert_ids.T, gate_weights.T],
        [array((rows, width + LANES))],
    )
    b1, z4, z8 = swap(labelled, 1), swap(labelled, 4), swap(labelled, 8)
    p0 = [labelled, b1]
    (sent,) = partials(p0)
    y0 = cross(sent)
    meet()
    (b4,) = relay([z4])
    b5, x6 = swap(b4, 1), swap(b4, 2)
    gap()
    gap()
    p1 = [b4, b5]
    (sent,) = partials(p1)
    y1 = cross(sent)
    note = swap(tail[0], 1)
    (h0,) = hidden(p0, y0)
    tail.append(note)
    (b6,) = relay([x6])
    b7 = swap(b6, 1)
    (b8,) = relay([z8])
    x10 = swap(b8, 2)
    p2 = [b6, b7]
    (sent,) = partials(p2, [h0])
    y2 = cross(sent)
    (h1,) = hidden(p1, y1)
    (again,) = relay([labelled])
    z12 = swap(again, 12)
    (b8,) = relay([b8, x10])
    b9 = swap(b8, 1)
    gap()
    p3 = [b8, b9]
    (sent,) = partials(p3, [h1])
    y3 = cross(sent)
    (again,) = relay([labelled])
    x2 = swap(again, 2)
    (h2,) = hidden(p2, y2)
    c0, c1 = outputs(p0, h0, y2, 4 * rows, rows)
    (b12,) = relay([z12])
    x14 = swap(b12, 2)
    (total,) = add([c0, c1], (whole, wide))
    (b12,) = relay([b12, x14])
    b13 = swap(b12, 1)
    gap()
    p4 = [b12, b13]
    (sent,) = partials(p4, [h2])
    y4 = cross(sent)
    (b2,) = relay([x2])
    b3 = swap(b2, 1)
    (h3,) = hidden(p3, y3)
    t3 = cross(h3)
    c4, c5 = outputs(p1, h1, y3, 8 * rows, rows)
    gap()
    (sent,) = add([c4, c5], (whole, one))
    s4 = swap(sent, 4)
    (latera,) = partials([b3])
    (later,) = partials([b2])
    (h4,) = hidden(p4, y4)
    t4 = cross(h4)
    (latera,) = relay([latera])
    y5a = cross(latera)
    (later,) = relay([later])
    y5 = cross(later)
    c6, c7 = outputs(p2, h2, y4, 8 * rows, rows)
    (total,) = add([total, s4], (whole, wide))
    gap()
    (sent,) = add([c6, c7], (whole, one))
    s6 = swap(sent, 6)
    c8, c9 = outputs(p3, h3, t3, 0, 2 * rows)
    gap()
    kept8, sent = add([c8, c9], (whole, wide), ([(0, rows), (1, rows)], one))
    x10 = swap(sent, 2)
    c12, c13 = outputs(p4, h4, t4, 0, 2 * rows)
    (total,) = add([total, s6], (whole, wide))
    (h5a,) = hidden([b3], y5a)
    t5a = cross(h5a)
    kept12, sent = add([c12, c13], (whole, wide), ([(0, rows), (1, rows)], one))
    x14 = swap(sent, 2)
    (sent,) = add([kept8, x10], (whole, one))
    s8 = swap(sent, 8)
    _, c3 = outputs([b3], h5a, t5a, 0, 0)
    (h5,) = hidden([b2], y5)
    t5 = cross(h5)
    (sent,) = add([kept12, x14], (whole, one))
    s12 = swap(sent, 12)
    c2, _ = outputs([b2], h5, t5, 0, rows)
    gap()
    (sent,) = add([c2, c3], (whole, one))
    s2 = swap(sent, 2)
    (total,) = add([total, s8], (whole, wide))
    (total,) = add([total, s12, s2], (whole + [(2, 0)], one))
    return total


def solution(mesh):
    placed = (
        P("expert", "dp"),
        P("expert", None),
        P("expert", None),
        P("expert", "dp", None),
        P("expert", "dp", None),
        P("expert", None, "dp"),
    )

    def body(tokens, expert_ids, gate_weights, gate_proj, up_proj, down_proj):
        tok_count, top_count = expert_ids.shape
        sources = lax.axis_size("expert")
        whole_blocks = 2 * tok_count * top_count >= sources * tok_count
        paired = lax.axis_size("dp") == 2 and sources == 16
        plan = gather_body if whole_blocks and paired else dispatch_body
        return plan(tokens, expert_ids, gate_weights, gate_proj, up_proj, down_proj)

    return jax.shard_map(
        body, mesh=mesh, in_specs=placed, out_specs=P("expert", "dp"), check_vma=False
    )
```

```python
import functools

import jax
import jax.numpy as jnp
from jax import lax
from jax.experimental import pallas as pl
from jax.experimental.pallas import tpu as pltpu
from jax.sharding import PartitionSpec as P


def block_places(block_ids, expert_count, capacity):
    tok_count, top_count = block_ids.shape
    flat_ids = block_ids.reshape(tok_count * top_count)
    matches = (flat_ids[:, None] == jnp.arange(expert_count, dtype=jnp.int32)[None, :]).astype(
        jnp.int32
    )
    earlier = jnp.cumsum(matches, axis=0) - matches
    slot_index = jnp.sum(earlier * matches, axis=1)
    return (flat_ids * capacity + slot_index).reshape(tok_count, top_count)


def dispatch_body(tokens, expert_ids, gate_weights, gate_proj, up_proj, down_proj):
    tok_count, top_count = expert_ids.shape
    row_width = tokens.shape[1]
    sources = lax.axis_size("expert")
    capacity = 2 * tok_count * top_count // sources
    positions = jnp.arange(sources * capacity, dtype=jnp.int32)
    places = block_places(expert_ids, sources, capacity)
    matches = places[:, :, None] == positions[None, None, :]
    weighting = jnp.sum(jnp.where(matches, gate_weights[:, :, None], 0.0), axis=1)
    chosen = jnp.any(matches, axis=1).astype(jnp.bfloat16)
    outgoing = lax.dot_general(
        chosen, tokens, (((0,), (0,)), ((), ())), preferred_element_type=jnp.float32
    ).astype(jnp.bfloat16)
    incoming = lax.all_to_all(
        outgoing.reshape(sources, capacity, row_width),
        "expert",
        split_axis=0,
        concat_axis=0,
        tiled=True,
    )
    expert_rows = incoming.reshape(sources * capacity, row_width)
    gate_part = jnp.dot(expert_rows, gate_proj[0], preferred_element_type=jnp.float32)
    up_part = jnp.dot(expert_rows, up_proj[0], preferred_element_type=jnp.float32)
    gate_sum, up_sum = (
        lax.psum(gate_part.astype(jnp.bfloat16), "dp").astype(jnp.float32),
        lax.psum(up_part.astype(jnp.bfloat16), "dp").astype(jnp.float32),
    )
    hidden = (jax.nn.silu(gate_sum) * up_sum).astype(jnp.bfloat16)
    expert_out = jnp.dot(hidden, down_proj[0], preferred_element_type=jnp.float32).astype(
        jnp.bfloat16
    )
    returned = lax.all_to_all(
        expert_out.reshape(sources, capacity, row_width),
        "expert",
        split_axis=0,
        concat_axis=0,
        tiled=True,
    )
    returned_flat = returned.reshape(sources * capacity, row_width)
    weight_high = weighting.astype(jnp.bfloat16)
    weight_low = (weighting - weight_high.astype(jnp.float32)).astype(jnp.bfloat16)
    combined = jnp.dot(weight_high, returned_flat, preferred_element_type=jnp.float32)
    combined = combined + jnp.dot(weight_low, returned_flat, preferred_element_type=jnp.float32)
    return combined.astype(jnp.bfloat16)


LANES = 128
VMEM_LIMIT = 10 * 1024 * 1024
TOKEN = jax.ShapeDtypeStruct((8, LANES), jnp.float32)
HERE = pl.BlockSpec(memory_space=pltpu.VMEM)


def call(kernel, inputs, outputs, after, scratch=(), relays=()):
    inputs = [v if isinstance(v, tuple) else (v, HERE) for v in inputs]
    flat = [value for group in relays for value in group]
    joined = [
        jax.ShapeDtypeStruct((sum(v.shape[0] for v in group),) + group[0].shape[1:], group[0].dtype)
        for group in relays
    ]

    def run(*refs):
        refs = list(refs)
        taken = [refs.pop(0) for _ in inputs]
        carried = [refs.pop(0) for _ in flat]
        del refs[: len(after)]
        made = [refs.pop(0) for _ in outputs]
        joined_refs = [refs.pop(0) for _ in joined]
        token_ref = refs.pop(0)
        token_ref[...] = jnp.zeros(token_ref.shape, token_ref.dtype)
        for group, out_ref in zip(relays, joined_refs, strict=True):
            start = 0
            for _ in group:
                piece = carried.pop(0)
                out_ref[start : start + piece.shape[0], :] = piece[...]
                start += piece.shape[0]
        if kernel is not None:
            kernel(*taken, *made, *refs)

    results = pl.pallas_call(
        run,
        in_specs=[spec for _, spec in inputs] + [HERE] * len(flat) + [pl.BlockSpec(memory_space=pl.ANY)] * len(after),
        out_specs=[HERE] * (len(outputs) + len(joined) + 1),
        out_shape=list(outputs) + joined + [TOKEN],
        scratch_shapes=list(scratch),
        compiler_params=pltpu.CompilerParams(vmem_limit_bytes=VMEM_LIMIT),
        cost_estimate=pl.CostEstimate(flops=8_000_000_000, bytes_accessed=1, transcendentals=0),
    )(*[value for value, _ in inputs], *flat, *after)
    return results[:-1], results[-1]


def label_kernel(sources, tokens_ref, ids_ref, weights_ref, out_ref):
    rows, width = tokens_ref.shape
    out_ref[:, :width] = tokens_ref[...]
    place = lax.broadcasted_iota(jnp.int32, (LANES, rows), 0)
    weight = jnp.zeros((LANES, rows), jnp.float32)
    for k in range(ids_ref.shape[0]):
        weight += jnp.where(ids_ref[k : k + 1, :] == place % sources, weights_ref[k : k + 1, :], 0.0)
    high = weight.astype(jnp.bfloat16).astype(jnp.float32)
    mid = (weight - high).astype(jnp.bfloat16).astype(jnp.float32)
    low = weight - high - mid
    term = place // sources
    picked = jnp.where(term == 0, high, jnp.where(term == 1, mid, jnp.where(term == 2, low, 0.0)))
    out_ref[:, width:] = jnp.transpose(picked).astype(jnp.bfloat16)


def collect(piece_refs, width, chunk_ref):
    start = 0
    for piece in piece_refs:
        chunk_ref[start : start + piece.shape[0], :] = piece[:, :width]
        start += piece.shape[0]


def partial_kernel(pieces, riders, tile, *refs):
    gate_ref, up_ref, *rider_refs, out_ref, chunk_ref = refs[pieces:]
    rows, width = chunk_ref.shape
    half = out_ref.shape[1]
    column = (1 - lax.axis_index("dp")) * half
    collect(refs[:pieces], width, chunk_ref)
    start = 2 * rows
    for ref in rider_refs:
        out_ref[start : start + ref.shape[0], :] = ref[...]
        start += ref.shape[0]

    @pl.loop(0, half // tile)
    def _(n):
        here = pl.ds(pl.multiple_of(column + n * tile, LANES), tile)
        there = pl.ds(pl.multiple_of(n * tile, LANES), tile)
        for i, ref in enumerate((gate_ref, up_ref)):
            part = jnp.dot(chunk_ref[...], ref[0, :, here], preferred_element_type=jnp.float32)
            out_ref[i * rows : (i + 1) * rows, there] = part.astype(jnp.bfloat16)


def hidden_kernel(pieces, tile, *refs):
    gate_ref, up_ref, arrived_ref, out_ref, chunk_ref = refs[pieces:]
    rows, width = chunk_ref.shape
    half = out_ref.shape[1]
    column = lax.axis_index("dp") * half
    collect(refs[:pieces], width, chunk_ref)

    @pl.loop(0, half // tile)
    def _(n):
        here = pl.ds(pl.multiple_of(column + n * tile, LANES), tile)
        there = pl.ds(pl.multiple_of(n * tile, LANES), tile)
        gate_sum, up_sum = (
            jnp.dot(chunk_ref[...], ref[0, :, here], preferred_element_type=jnp.float32)
            + arrived_ref[i * rows : (i + 1) * rows, there].astype(jnp.float32)
            for i, ref in enumerate((gate_ref, up_ref))
        )
        out_ref[:, there] = (gate_sum / (1.0 + jnp.exp(-gate_sum)) * up_sum).astype(jnp.bfloat16)


def output_kernel(pieces, sources, tile, behind, *refs):
    mine_ref, other_ref, down_ref = refs[pieces : pieces + 3]
    *out_refs, weight_ref = refs[pieces + 3 :]
    start = 0
    for piece in refs[:pieces]:
        rows = piece.shape[0]
        lane = lax.broadcasted_iota(jnp.int32, (rows, LANES), 1)
        label = piece[:, piece.shape[1] - LANES :].astype(jnp.float32)
        terms = jnp.where(lane % sources == lax.axis_index("expert"), label, 0.0)
        weight_ref[start : start + rows, :] = jnp.sum(terms, axis=1, keepdims=True)
        start += rows
    count, half = mine_ref.shape
    other = other_ref[behind : behind + count, :]
    first = lax.axis_index("dp") * half
    mine_rows = pl.ds(pl.multiple_of(first, LANES), half)
    other_rows = pl.ds(pl.multiple_of(half - first, LANES), half)

    @pl.loop(0, down_ref.shape[2] // tile)
    def _(n):
        here = pl.ds(pl.multiple_of(n * tile, LANES), tile)
        out = jnp.dot(mine_ref[...], down_ref[0, mine_rows, here], preferred_element_type=jnp.float32)
        out += jnp.dot(other, down_ref[0, other_rows, here], preferred_element_type=jnp.float32)
        out *= weight_ref[...]
        start = 0
        for ref in out_refs:
            ref[:, here] = out[start : start + ref.shape[0]].astype(ref.dtype)
            start += ref.shape[0]


def add_kernel(sums, *refs):
    inputs = 1 + max(i for terms in sums for i, _ in terms)
    for terms, out_ref in zip(sums, refs[inputs:], strict=True):
        rows = out_ref.shape[0]
        total = None
        for i, start in terms:
            value = refs[i][start : start + rows, :].astype(jnp.float32)
            total = value if total is None else total + value
        out_ref[...] = total.astype(out_ref.dtype)


def gather_body(tokens, expert_ids, gate_weights, gate_proj, up_proj, down_proj):
    rows, width = tokens.shape
    sources = lax.axis_size("expert")
    half = gate_proj.shape[2] // 2
    tile = half
    out_tile = 1024 if width % 1024 == 0 else width

    def swap(value, r):
        return lax.ppermute(value, "expert", [(i, i ^ r) for i in range(sources)])

    def cross(value):
        return lax.ppermute(value, "dp", [(0, 1), (1, 0)])

    def array(shape, dtype=jnp.bfloat16):
        return jax.ShapeDtypeStruct(shape, dtype)

    tail = [jnp.zeros(TOKEN.shape, TOKEN.dtype)]

    def step(kernel, inputs, outputs, scratch=(), relays=()):
        results, token = call(kernel, inputs, outputs, list(tail), scratch, relays)
        tail[:] = [token]
        return results

    def count(pieces):
        return sum(p.shape[0] for p in pieces)

    def partials(pieces, riders=(), relays=()):
        total = count(pieces)
        sent, *relayed = step(
            functools.partial(partial_kernel, len(pieces), len(riders), tile),
            [*pieces, gate_proj, up_proj, *riders],
            [array((2 * total + count(riders), half))],
            [pltpu.VMEM((total, width), jnp.bfloat16)],
            relays,
        )
        return sent, *relayed

    def hidden(pieces, arrived, relays=()):
        total = count(pieces)
        mine, *relayed = step(
            functools.partial(hidden_kernel, len(pieces), tile),
            [*pieces, gate_proj, up_proj, arrived],
            [array((total, half))],
            [pltpu.VMEM((total, width), jnp.bfloat16)],
            relays,
        )
        return mine, *relayed

    def outputs(pieces, mine, arrived, behind, even, relays=()):
        total = count(pieces)
        made = [array((even, width), jnp.float32)] if even else []
        made += [array((total - even, width))] if total > even else []
        results = step(
            functools.partial(output_kernel, len(pieces), sources, out_tile, behind),
            [*pieces, mine, arrived, down_proj],
            made,
            [pltpu.VMEM((total, 1), jnp.float32)],
            relays,
        )
        kept = results[0] if even else None
        back = swap(results[len(made) - 1], 1) if total > even else None
        return kept, back, *results[len(made) :]

    def add(values, *sums, relays=()):
        return step(
            functools.partial(add_kernel, [terms for terms, _ in sums]),
            values,
            [shape for _, shape in sums],
            relays=relays,
        )

    def relay(*groups):
        return step(None, [], [], relays=[list(g) for g in groups])

    one, two, wide = array((rows, width)), array((2 * rows, width)), array((rows, width), jnp.float32)
    whole = [(0, 0), (1, 0)]

    def gap():
        step(None, [], [])

    def meet():
        tail.append(swap(tail[0], 1))

    (labelled,) = step(
        functools.partial(label_kernel, sources),
        [tokens, expert_ids.T, gate_weights.T],
        [array((rows, width + LANES))],
    )
    b1, z4, z8 = swap(labelled, 1), swap(labelled, 4), swap(labelled, 8)
    p0 = [labelled, b1]
    (sent,) = partials(p0)
    y0 = cross(sent)
    meet()
    (b4,) = relay([z4])
    b5, x6 = swap(b4, 1), swap(b4, 2)
    gap()
    gap()
    p1 = [b4, b5]
    (sent,) = partials(p1)
    y1 = cross(sent)
    note = swap(tail[0], 1)
    (h0,) = hidden(p0, y0)
    tail.append(note)
    (b6,) = relay([x6])
    b7 = swap(b6, 1)
    (b8,) = relay([z8])
    x10 = swap(b8, 2)
    p2 = [b6, b7]
    (sent,) = partials(p2, [h0])
    y2 = cross(sent)
    (h1,) = hidden(p1, y1)
    (again,) = relay([labelled])
    z12 = swap(again, 12)
    (b8,) = relay([b8, x10])
    b9 = swap(b8, 1)
    gap()
    p3 = [b8, b9]
    (sent,) = partials(p3, [h1])
    y3 = cross(sent)
    (again,) = relay([labelled])
    x2 = swap(again, 2)
    (h2,) = hidden(p2, y2)
    c0, c1 = outputs(p0, h0, y2, 4 * rows, rows)
    (b12,) = relay([z12])
    x14 = swap(b12, 2)
    (total,) = add([c0, c1], (whole, wide))
    (b12,) = relay([b12, x14])
    b13 = swap(b12, 1)
    gap()
    p4 = [b12, b13]
    (sent,) = partials(p4, [h2])
    y4 = cross(sent)
    (b2,) = relay([x2])
    b3 = swap(b2, 1)
    (h3,) = hidden(p3, y3)
    t3 = cross(h3)
    c4, c5 = outputs(p1, h1, y3, 8 * rows, rows)
    gap()
    (sent,) = add([c4, c5], (whole, one))
    s4 = swap(sent, 4)
    (latera,) = partials([b3])
    (later,) = partials([b2])
    (h4,) = hidden(p4, y4)
    t4 = cross(h4)
    (latera,) = relay([latera])
    y5a = cross(latera)
    (later,) = relay([later])
    y5 = cross(later)
    c6, c7 = outputs(p2, h2, y4, 8 * rows, rows)
    (total,) = add([total, s4], (whole, wide))
    gap()
    (sent,) = add([c6, c7], (whole, one))
    s6 = swap(sent, 6)
    c8, c9 = outputs(p3, h3, t3, 0, 2 * rows)
    gap()
    kept8, sent = add([c8, c9], (whole, wide), ([(0, rows), (1, rows)], one))
    x10 = swap(sent, 2)
    c12, c13 = outputs(p4, h4, t4, 0, 2 * rows)
    (total,) = add([total, s6], (whole, wide))
    (h5a,) = hidden([b3], y5a)
    t5a = cross(h5a)
    kept12, sent = add([c12, c13], (whole, wide), ([(0, rows), (1, rows)], one))
    x14 = swap(sent, 2)
    (sent,) = add([kept8, x10], (whole, one))
    s8 = swap(sent, 8)
    _, c3 = outputs([b3], h5a, t5a, 0, 0)
    (h5,) = hidden([b2], y5)
    t5 = cross(h5)
    (sent,) = add([kept12, x14], (whole, one))
    s12 = swap(sent, 12)
    c2, _ = outputs([b2], h5, t5, 0, rows)
    gap()
    (sent,) = add([c2, c3], (whole, one))
    s2 = swap(sent, 2)
    (total,) = add([total, s8], (whole, wide))
    (total,) = add([total, s12, s2], (whole + [(2, 0)], one))
    return total


def solution(mesh):
    placed = (
        P("expert", "dp"),
        P("expert", None),
        P("expert", None),
        P("expert", "dp", None),
        P("expert", "dp", None),
        P("expert", None, "dp"),
    )

    def body(tokens, expert_ids, gate_weights, gate_proj, up_proj, down_proj):
        tok_count, top_count = expert_ids.shape
        sources = lax.axis_size("expert")
        whole_blocks = 2 * tok_count * top_count >= sources * tok_count
        paired = lax.axis_size("dp") == 2 and sources == 16
        plan = gather_body if whole_blocks and paired else dispatch_body
        return plan(tokens, expert_ids, gate_weights, gate_proj, up_proj, down_proj)

    return jax.shard_map(
        body, mesh=mesh, in_specs=placed, out_specs=P("expert", "dp"), check_vma=False
    )
```

```python
import functools

import jax
import jax.numpy as jnp
from jax import lax
from jax.experimental import pallas as pl
from jax.experimental.pallas import tpu as pltpu
from jax.sharding import PartitionSpec as P


def block_places(block_ids, expert_count, capacity):
    tok_count, top_count = block_ids.shape
    flat_ids = block_ids.reshape(tok_count * top_count)
    matches = (flat_ids[:, None] == jnp.arange(expert_count, dtype=jnp.int32)[None, :]).astype(
        jnp.int32
    )
    earlier = jnp.cumsum(matches, axis=0) - matches
    slot_index = jnp.sum(earlier * matches, axis=1)
    return (flat_ids * capacity + slot_index).reshape(tok_count, top_count)


def dispatch_body(tokens, expert_ids, gate_weights, gate_proj, up_proj, down_proj):
    tok_count, top_count = expert_ids.shape
    row_width = tokens.shape[1]
    sources = lax.axis_size("expert")
    capacity = 2 * tok_count * top_count // sources
    positions = jnp.arange(sources * capacity, dtype=jnp.int32)
    places = block_places(expert_ids, sources, capacity)
    matches = places[:, :, None] == positions[None, None, :]
    weighting = jnp.sum(jnp.where(matches, gate_weights[:, :, None], 0.0), axis=1)
    chosen = jnp.any(matches, axis=1).astype(jnp.bfloat16)
    outgoing = lax.dot_general(
        chosen, tokens, (((0,), (0,)), ((), ())), preferred_element_type=jnp.float32
    ).astype(jnp.bfloat16)
    incoming = lax.all_to_all(
        outgoing.reshape(sources, capacity, row_width),
        "expert",
        split_axis=0,
        concat_axis=0,
        tiled=True,
    )
    expert_rows = incoming.reshape(sources * capacity, row_width)
    gate_part = jnp.dot(expert_rows, gate_proj[0], preferred_element_type=jnp.float32)
    up_part = jnp.dot(expert_rows, up_proj[0], preferred_element_type=jnp.float32)
    gate_sum, up_sum = (
        lax.psum(gate_part.astype(jnp.bfloat16), "dp").astype(jnp.float32),
        lax.psum(up_part.astype(jnp.bfloat16), "dp").astype(jnp.float32),
    )
    hidden = (jax.nn.silu(gate_sum) * up_sum).astype(jnp.bfloat16)
    expert_out = jnp.dot(hidden, down_proj[0], preferred_element_type=jnp.float32).astype(
        jnp.bfloat16
    )
    returned = lax.all_to_all(
        expert_out.reshape(sources, capacity, row_width),
        "expert",
        split_axis=0,
        concat_axis=0,
        tiled=True,
    )
    returned_flat = returned.reshape(sources * capacity, row_width)
    weight_high = weighting.astype(jnp.bfloat16)
    weight_low = (weighting - weight_high.astype(jnp.float32)).astype(jnp.bfloat16)
    combined = jnp.dot(weight_high, returned_flat, preferred_element_type=jnp.float32)
    combined = combined + jnp.dot(weight_low, returned_flat, preferred_element_type=jnp.float32)
    return combined.astype(jnp.bfloat16)


LANES = 128
VMEM_LIMIT = 10 * 1024 * 1024
TOKEN = jax.ShapeDtypeStruct((8, LANES), jnp.float32)
HERE = pl.BlockSpec(memory_space=pltpu.VMEM)


def call(kernel, inputs, outputs, after, scratch=(), relays=()):
    inputs = [v if isinstance(v, tuple) else (v, HERE) for v in inputs]
    flat = [value for group in relays for value in group]
    joined = [
        jax.ShapeDtypeStruct((sum(v.shape[0] for v in group),) + group[0].shape[1:], group[0].dtype)
        for group in relays
    ]

    def run(*refs):
        refs = list(refs)
        taken = [refs.pop(0) for _ in inputs]
        carried = [refs.pop(0) for _ in flat]
        del refs[: len(after)]
        made = [refs.pop(0) for _ in outputs]
        joined_refs = [refs.pop(0) for _ in joined]
        token_ref = refs.pop(0)
        token_ref[...] = jnp.zeros(token_ref.shape, token_ref.dtype)
        for group, out_ref in zip(relays, joined_refs, strict=True):
            start = 0
            for _ in group:
                piece = carried.pop(0)
                out_ref[start : start + piece.shape[0], :] = piece[...]
                start += piece.shape[0]
        if kernel is not None:
            kernel(*taken, *made, *refs)

    results = pl.pallas_call(
        run,
        in_specs=[spec for _, spec in inputs] + [HERE] * len(flat) + [pl.BlockSpec(memory_space=pl.ANY)] * len(after),
        out_specs=[HERE] * (len(outputs) + len(joined) + 1),
        out_shape=list(outputs) + joined + [TOKEN],
        scratch_shapes=list(scratch),
        compiler_params=pltpu.CompilerParams(vmem_limit_bytes=VMEM_LIMIT),
        cost_estimate=pl.CostEstimate(flops=8_000_000_000, bytes_accessed=1, transcendentals=0),
    )(*[value for value, _ in inputs], *flat, *after)
    return results[:-1], results[-1]


def label_kernel(sources, tokens_ref, ids_ref, weights_ref, out_ref):
    rows, width = tokens_ref.shape
    out_ref[:, :width] = tokens_ref[...]
    place = lax.broadcasted_iota(jnp.int32, (LANES, rows), 0)
    weight = jnp.zeros((LANES, rows), jnp.float32)
    for k in range(ids_ref.shape[0]):
        weight += jnp.where(ids_ref[k : k + 1, :] == place % sources, weights_ref[k : k + 1, :], 0.0)
    high = weight.astype(jnp.bfloat16).astype(jnp.float32)
    mid = (weight - high).astype(jnp.bfloat16).astype(jnp.float32)
    low = weight - high - mid
    term = place // sources
    picked = jnp.where(term == 0, high, jnp.where(term == 1, mid, jnp.where(term == 2, low, 0.0)))
    out_ref[:, width:] = jnp.transpose(picked).astype(jnp.bfloat16)


def collect(piece_refs, width, chunk_ref):
    start = 0
    for piece in piece_refs:
        chunk_ref[start : start + piece.shape[0], :] = piece[:, :width]
        start += piece.shape[0]


def partial_kernel(pieces, riders, tile, *refs):
    gate_ref, up_ref, *rider_refs, out_ref, chunk_ref = refs[pieces:]
    rows, width = chunk_ref.shape
    half = out_ref.shape[1]
    column = (1 - lax.axis_index("dp")) * half
    collect(refs[:pieces], width, chunk_ref)
    start = 2 * rows
    for ref in rider_refs:
        out_ref[start : start + ref.shape[0], :] = ref[...]
        start += ref.shape[0]

    @pl.loop(0, half // tile)
    def _(n):
        here = pl.ds(pl.multiple_of(column + n * tile, LANES), tile)
        there = pl.ds(pl.multiple_of(n * tile, LANES), tile)
        for i, ref in enumerate((gate_ref, up_ref)):
            part = jnp.dot(chunk_ref[...], ref[0, :, here], preferred_element_type=jnp.float32)
            out_ref[i * rows : (i + 1) * rows, there] = part.astype(jnp.bfloat16)


def hidden_kernel(pieces, tile, *refs):
    gate_ref, up_ref, arrived_ref, out_ref, chunk_ref = refs[pieces:]
    rows, width = chunk_ref.shape
    half = out_ref.shape[1]
    column = lax.axis_index("dp") * half
    collect(refs[:pieces], width, chunk_ref)

    @pl.loop(0, half // tile)
    def _(n):
        here = pl.ds(pl.multiple_of(column + n * tile, LANES), tile)
        there = pl.ds(pl.multiple_of(n * tile, LANES), tile)
        gate_sum, up_sum = (
            jnp.dot(chunk_ref[...], ref[0, :, here], preferred_element_type=jnp.float32)
            + arrived_ref[i * rows : (i + 1) * rows, there].astype(jnp.float32)
            for i, ref in enumerate((gate_ref, up_ref))
        )
        out_ref[:, there] = (gate_sum / (1.0 + jnp.exp(-gate_sum)) * up_sum).astype(jnp.bfloat16)


def output_kernel(pieces, sources, tile, behind, *refs):
    mine_ref, other_ref, down_ref = refs[pieces : pieces + 3]
    *out_refs, weight_ref = refs[pieces + 3 :]
    start = 0
    for piece in refs[:pieces]:
        rows = piece.shape[0]
        lane = lax.broadcasted_iota(jnp.int32, (rows, LANES), 1)
        label = piece[:, piece.shape[1] - LANES :].astype(jnp.float32)
        terms = jnp.where(lane % sources == lax.axis_index("expert"), label, 0.0)
        weight_ref[start : start + rows, :] = jnp.sum(terms, axis=1, keepdims=True)
        start += rows
    count, half = mine_ref.shape
    other = other_ref[behind : behind + count, :]
    first = lax.axis_index("dp") * half
    mine_rows = pl.ds(pl.multiple_of(first, LANES), half)
    other_rows = pl.ds(pl.multiple_of(half - first, LANES), half)

    @pl.loop(0, down_ref.shape[2] // tile)
    def _(n):
        here = pl.ds(pl.multiple_of(n * tile, LANES), tile)
        out = jnp.dot(mine_ref[...], down_ref[0, mine_rows, here], preferred_element_type=jnp.float32)
        out += jnp.dot(other, down_ref[0, other_rows, here], preferred_element_type=jnp.float32)
        out *= weight_ref[...]
        start = 0
        for ref in out_refs:
            ref[:, here] = out[start : start + ref.shape[0]].astype(ref.dtype)
            start += ref.shape[0]


def add_kernel(sums, *refs):
    inputs = 1 + max(i for terms in sums for i, _ in terms)
    for terms, out_ref in zip(sums, refs[inputs:], strict=True):
        rows = out_ref.shape[0]
        total = None
        for i, start in terms:
            value = refs[i][start : start + rows, :].astype(jnp.float32)
            total = value if total is None else total + value
        out_ref[...] = total.astype(out_ref.dtype)


def gather_body(tokens, expert_ids, gate_weights, gate_proj, up_proj, down_proj):
    rows, width = tokens.shape
    sources = lax.axis_size("expert")
    half = gate_proj.shape[2] // 2
    tile = half
    out_tile = width

    def swap(value, r):
        return lax.ppermute(value, "expert", [(i, i ^ r) for i in range(sources)])

    def cross(value):
        return lax.ppermute(value, "dp", [(0, 1), (1, 0)])

    def array(shape, dtype=jnp.bfloat16):
        return jax.ShapeDtypeStruct(shape, dtype)

    tail = [jnp.zeros(TOKEN.shape, TOKEN.dtype)]

    def step(kernel, inputs, outputs, scratch=(), relays=()):
        results, token = call(kernel, inputs, outputs, list(tail), scratch, relays)
        tail[:] = [token]
        return results

    def count(pieces):
        return sum(p.shape[0] for p in pieces)

    def partials(pieces, riders=(), relays=()):
        total = count(pieces)
        sent, *relayed = step(
            functools.partial(partial_kernel, len(pieces), len(riders), tile),
            [*pieces, gate_proj, up_proj, *riders],
            [array((2 * total + count(riders), half))],
            [pltpu.VMEM((total, width), jnp.bfloat16)],
            relays,
        )
        return sent, *relayed

    def hidden(pieces, arrived, relays=()):
        total = count(pieces)
        mine, *relayed = step(
            functools.partial(hidden_kernel, len(pieces), tile),
            [*pieces, gate_proj, up_proj, arrived],
            [array((total, half))],
            [pltpu.VMEM((total, width), jnp.bfloat16)],
            relays,
        )
        return mine, *relayed

    def outputs(pieces, mine, arrived, behind, even, relays=()):
        total = count(pieces)
        made = [array((even, width), jnp.float32)] if even else []
        made += [array((total - even, width))] if total > even else []
        results = step(
            functools.partial(output_kernel, len(pieces), sources, out_tile, behind),
            [*pieces, mine, arrived, down_proj],
            made,
            [pltpu.VMEM((total, 1), jnp.float32)],
            relays,
        )
        kept = results[0] if even else None
        back = swap(results[len(made) - 1], 1) if total > even else None
        return kept, back, *results[len(made) :]

    def add(values, *sums, relays=()):
        return step(
            functools.partial(add_kernel, [terms for terms, _ in sums]),
            values,
            [shape for _, shape in sums],
            relays=relays,
        )

    def relay(*groups):
        return step(None, [], [], relays=[list(g) for g in groups])

    one, two, wide = array((rows, width)), array((2 * rows, width)), array((rows, width), jnp.float32)
    whole = [(0, 0), (1, 0)]

    def gap():
        step(None, [], [])

    def meet():
        tail.append(swap(tail[0], 1))

    (labelled,) = step(
        functools.partial(label_kernel, sources),
        [tokens, expert_ids.T, gate_weights.T],
        [array((rows, width + LANES))],
    )
    b1, z4, z8 = swap(labelled, 1), swap(labelled, 4), swap(labelled, 8)
    p0 = [labelled, b1]
    (sent,) = partials(p0)
    y0 = cross(sent)
    meet()
    (b4,) = relay([z4])
    b5, x6 = swap(b4, 1), swap(b4, 2)
    gap()
    gap()
    p1 = [b4, b5]
    (sent,) = partials(p1)
    y1 = cross(sent)
    note = swap(tail[0], 1)
    (h0,) = hidden(p0, y0)
    tail.append(note)
    (b6,) = relay([x6])
    b7 = swap(b6, 1)
    (b8,) = relay([z8])
    x10 = swap(b8, 2)
    p2 = [b6, b7]
    (sent,) = partials(p2, [h0])
    y2 = cross(sent)
    (h1,) = hidden(p1, y1)
    (again,) = relay([labelled])
    z12 = swap(again, 12)
    (b8,) = relay([b8, x10])
    b9 = swap(b8, 1)
    gap()
    p3 = [b8, b9]
    (sent,) = partials(p3, [h1])
    y3 = cross(sent)
    (again,) = relay([labelled])
    x2 = swap(again, 2)
    (h2,) = hidden(p2, y2)
    c0, c1 = outputs(p0, h0, y2, 4 * rows, rows)
    (b12,) = relay([z12])
    x14 = swap(b12, 2)
    (total,) = add([c0, c1], (whole, wide))
    (b12,) = relay([b12, x14])
    b13 = swap(b12, 1)
    gap()
    p4 = [b12, b13]
    (sent,) = partials(p4, [h2])
    y4 = cross(sent)
    (b2,) = relay([x2])
    b3 = swap(b2, 1)
    (h3,) = hidden(p3, y3)
    t3 = cross(h3)
    c4, c5 = outputs(p1, h1, y3, 8 * rows, rows)
    gap()
    (sent,) = add([c4, c5], (whole, one))
    s4 = swap(sent, 4)
    (latera,) = partials([b3])
    (later,) = partials([b2])
    (h4,) = hidden(p4, y4)
    t4 = cross(h4)
    (latera,) = relay([latera])
    y5a = cross(latera)
    (later,) = relay([later])
    y5 = cross(later)
    c6, c7 = outputs(p2, h2, y4, 8 * rows, rows)
    (total,) = add([total, s4], (whole, wide))
    gap()
    (sent,) = add([c6, c7], (whole, one))
    s6 = swap(sent, 6)
    c8, c9 = outputs(p3, h3, t3, 0, 2 * rows)
    gap()
    kept8, sent = add([c8, c9], (whole, wide), ([(0, rows), (1, rows)], one))
    x10 = swap(sent, 2)
    c12, c13 = outputs(p4, h4, t4, 0, 2 * rows)
    (total,) = add([total, s6], (whole, wide))
    (h5a,) = hidden([b3], y5a)
    t5a = cross(h5a)
    kept12, sent = add([c12, c13], (whole, wide), ([(0, rows), (1, rows)], one))
    x14 = swap(sent, 2)
    (sent,) = add([kept8, x10], (whole, one))
    s8 = swap(sent, 8)
    _, c3 = outputs([b3], h5a, t5a, 0, 0)
    (h5,) = hidden([b2], y5)
    t5 = cross(h5)
    (sent,) = add([kept12, x14], (whole, one))
    s12 = swap(sent, 12)
    c2, _ = outputs([b2], h5, t5, 0, rows)
    gap()
    (sent,) = add([c2, c3], (whole, one))
    s2 = swap(sent, 2)
    (total,) = add([total, s8], (whole, wide))
    (total,) = add([total, s12, s2], (whole + [(2, 0)], one))
    return total


def solution(mesh):
    placed = (
        P("expert", "dp"),
        P("expert", None),
        P("expert", None),
        P("expert", "dp", None),
        P("expert", "dp", None),
        P("expert", None, "dp"),
    )

    def body(tokens, expert_ids, gate_weights, gate_proj, up_proj, down_proj):
        tok_count, top_count = expert_ids.shape
        sources = lax.axis_size("expert")
        whole_blocks = 2 * tok_count * top_count >= sources * tok_count
        paired = lax.axis_size("dp") == 2 and sources == 16
        plan = gather_body if whole_blocks and paired else dispatch_body
        return plan(tokens, expert_ids, gate_weights, gate_proj, up_proj, down_proj)

    return jax.shard_map(
        body, mesh=mesh, in_specs=placed, out_specs=P("expert", "dp"), check_vma=False
    )
```
